32 devices in a mesh: groups: 2 (over x), ta: 16 (over z, y, core).
Axes of the slice: x: 2, y: 2, z: 4, core: 2. Of those that a mesh axis runs over, the one named last changes fastest.
Arguments:
- out_field: float32 [16, 64, 1024], P(None, ('groups', 'ta')), parts along dimension 1, may hold values from -6 to 6
- out_cot: float32 [16, 64, 1024], P(None, ('groups', 'ta')), parts along dimension 1, may hold values from -6 to 6
- jac_cot: float32 [64, 1024], P(('groups', 'ta')), parts along dimension 0, may hold values from -6 to 6
- mask: int32 [64, 1024], P(('groups', 'ta')), parts along dimension 0, may hold values 0 or 1
- perm: int32 [16], replicated, may hold values from 0 to 15, each once
- lower_param: float32 [16, 16], replicated, may hold values from -0.6 to 0.6
- upper_param: float32 [16, 16], replicated, may hold values from -0.6 to 0.6
- log_scale: float32 [16], replicated, may hold values from -0.3 to 0.3
- kern1: bfloat16 [81, 32, 16], replicated, may hold values from -0.15625 to 0.15625
- bias1: float32 [32], replicated, may hold values from -3 to 3
- kern2: bfloat16 [81, 32, 32], replicated, may hold values from -0.125 to 0.125
- bias2: float32 [32], replicated, may hold values from -2 to 2
Outputs:
- field_in: float32 [16, 64, 1024], P(None, ('groups', 'ta')), parts along dimension 1
- field_cot: float32 [16, 64, 1024], P(None, ('groups', 'ta')), parts along dimension 1
- grad_kern1: float32 [162, 32, 16], P('groups'), parts along dimension 0
- grad_bias1: float32 [64], P('groups'), parts along dimension 0
- grad_kern2: float32 [162, 32, 32], P('groups'), parts along dimension 0
- grad_bias2: float32 [64], P('groups'), parts along dimension 0
- grad_lower: float32 [32, 16], P('groups'), parts along dimension 0
- grad_upper: float32 [32, 16], P('groups'), parts along dimension 0
- grad_logs: float32 [32], P('groups'), parts along dimension 0
The draws below stay inside these ranges and needn't reach their ends.
There are 2 independent parts, one for each index of `groups`. The reference program is written for one: setup_inputs(seed, part) draws one part's arguments, and reference() takes and returns one part's arrays. A program takes and returns all parts, laid end to end along the dimension named above; an argument that names none is the same for every part. Nothing has to cross between parts.
Inputs may be any that keep to these rules, and one draw needn't show every extreme that they name: `perm`: each of 0 to 15 exactly once.
All inputs are finite; a program needn't handle non-finite values. No bound on the sum of `mask` on one device may be relied on, other than what follows from the above.
Results may differ from the reference program's by a relative error of at most 0.0076.
Values may be sent and summed in bfloat16 or wider, within the bound.
A program may use at most 64 MiB of HBM per device.

```python
import math
import jax
import jax.numpy as jnp
from jax import lax

C = 16
HID = 32
LX = 8
LY = 8
LZ = 16
S = 1024
NT = 32
SITES_ALL = 32768


def with_ends(array, key, smallest, high):
    extent = array.shape
    place = [jax.random.randint(jax.random.fold_in(key, axis), (), 0, extent[axis]) for axis in range(len(extent))]
    array = array.at[tuple(place)].set(smallest)
    longest = extent.index(max(extent))
    place[longest] = (place[longest] + 1) % extent[longest]
    return array.at[tuple(place)].set(high)


def block_levels(own_key, extent, split, low, top_value):
    factor_of = 1.0
    for position, parts in split:
        heights = jax.random.uniform(jax.random.fold_in(jax.random.fold_in(own_key, 6), position), (parts,), jnp.float32, low / len(split), top_value / len(split))
        factor_of = factor_of * jnp.repeat(jnp.exp(heights), extent[position] // parts).reshape((-1,) + (1,) * (len(extent) - 1 - position))
    return factor_of


def centred(rng, extent, spread, limit, pieces=(), kind=jnp.bfloat16):
    factor_of = block_levels(rng, extent, pieces, -0.22, 0.18) if pieces else 1.0
    array = jax.random.normal(rng, extent, jnp.float32) * spread * factor_of
    return jnp.minimum(jnp.maximum(array, -limit), limit).astype(kind)


def setup_inputs(seed: int = 0, part: int = 0) -> dict:
    key_of = jax.random.split(jax.random.key(seed), 13)
    own_keys = jax.random.split(jax.random.fold_in(key_of[12], part), 13)
    return {
        "out_field": centred(own_keys[0], (C, NT, S), 1.0, 6.0, ((1, 16),), jnp.float32),
        "out_cot": centred(own_keys[1], (C, NT, S), 1.0, 6.0, ((1, 16),), jnp.float32),
        "jac_cot": centred(own_keys[2], (NT, S), 1.0, 6.0, ((0, 16),), jnp.float32),
        "mask": with_ends((jax.random.randint(own_keys[3], (NT, S), 0, 2) < 1).astype(jnp.int32), jax.random.fold_in(own_keys[3], 1), 0, 1),
        "perm": jax.random.permutation(key_of[4], C).astype(jnp.int32),
        "lower_param": centred(key_of[5], (C, C), 0.15, 0.6, (), jnp.float32),
        "upper_param": centred(key_of[6], (C, C), 0.15, 0.6, (), jnp.float32),
        "log_scale": jnp.clip(jax.random.uniform(key_of[7], (C,), jnp.float32, -0.3, 0.3), -0.3, 0.3),
        "kern1": centred(key_of[8], (81, HID, C), (81 * C) ** -0.5, 0.15625),
        "bias1": centred(key_of[9], (HID,), 0.5, 3.0, (), jnp.float32),
        "kern2": centred(key_of[10], (81, 2 * C, HID), (81 * HID) ** -0.5, 0.125),
        "bias2": centred(key_of[11], (2 * C,), 0.3, 2.0, (), jnp.float32),
    }


HIGH = lax.Precision.HIGHEST

def nilpotent_inverse(nilpart):
    count = nilpart.shape[0]
    eye = jnp.eye(count, dtype=jnp.float32)
    result = eye - nilpart
    power = jnp.dot(nilpart, nilpart, precision=HIGH)
    span = 2
    while span < count:
        result = jnp.dot(result, eye + power, precision=HIGH)
        power = jnp.dot(power, power, precision=HIGH)
        span = span * 2
    return result

def lower_inverse(lower_tri):
    return nilpotent_inverse(jnp.tril(lower_tri, -1))

def upper_inverse(upper_tri):
    diag_vals = jnp.diagonal(upper_tri)
    scaled = jnp.triu(upper_tri, 1) / diag_vals[:, None]
    return nilpotent_inverse(scaled) * (1.0 / diag_vals)[None, :]

def all_offsets():
    listing = []
    for t_off in (-1, 0, 1):
        for x_off in (-1, 0, 1):
            for y_off in (-1, 0, 1):
                for z_off in (-1, 0, 1):
                    listing.append((t_off, x_off, y_off, z_off))
    return listing

def roll_field(values, offsets):
    return jnp.roll(values, shift=(-offsets[0], -offsets[1], -offsets[2], -offsets[3]), axis=(1, 2, 3, 4))

def conv_ref(values, kernel):
    kernel_f = kernel.astype(jnp.float32)
    total = None
    for tap_id, offsets in enumerate(all_offsets()):
        term = jnp.einsum('oi,itxyz->otxyz', kernel_f[tap_id], roll_field(values, offsets), precision=HIGH)
        total = term if total is None else total + term
    return total

def grads_ref(cotangent, values):
    blocks = []
    for offsets in all_offsets():
        blocks.append(jnp.einsum('otxyz,itxyz->oi', cotangent, roll_field(values, offsets), precision=HIGH))
    return jnp.stack(blocks)

def reference(out_field, out_cot, jac_cot, mask, perm, lower_param, upper_param, log_scale, kern1, bias1, kern2, bias2):
    chans = out_field.shape[0]
    slices = out_field.shape[1]
    shape5 = (chans, slices, LX, LY, LZ)
    eye = jnp.eye(chans, dtype=jnp.float32)
    permuter = (perm[:, None] == jnp.arange(chans, dtype=jnp.int32)[None, :]).astype(jnp.float32)
    lower_tri = jnp.tril(lower_param, -1) + eye
    upper_tri = jnp.triu(upper_param, 1) + jnp.diag(jnp.exp(log_scale))
    mixer = jnp.dot(jnp.dot(permuter, lower_tri, precision=HIGH), upper_tri, precision=HIGH)
    unmixer = jnp.dot(jnp.dot(upper_inverse(upper_tri), lower_inverse(lower_tri), precision=HIGH), permuter.T, precision=HIGH)
    flat_out = out_field.reshape(chans, -1)
    flat_coupled = jnp.dot(unmixer, flat_out, precision=HIGH)
    coupled = flat_coupled.reshape(shape5)
    keep = mask.reshape(shape5[1:]).astype(jnp.float32)[None]
    free_part = 1.0 - keep
    frozen = (keep * coupled).astype(jnp.bfloat16)
    frozen_f = frozen.astype(jnp.float32)
    hidden = jnp.tanh(conv_ref(frozen_f, kern1) + bias1[:, None, None, None, None]).astype(jnp.bfloat16)
    hidden_f = hidden.astype(jnp.float32)
    net_out = conv_ref(hidden_f, kern2) + bias2[:, None, None, None, None]
    scale_field = jnp.tanh(net_out[:chans])
    shift_field = net_out[chans:]
    field_in = keep * coupled + free_part * (coupled - shift_field) * jnp.exp(-scale_field)
    flat_cot = out_cot.reshape(chans, -1)
    coupled_cot = jnp.dot(mixer.T, flat_cot, precision=HIGH).reshape(shape5)
    mix_sum = jnp.dot(flat_cot, flat_coupled.T, precision=HIGH)
    jac_field = jac_cot.reshape(shape5[1:])[None]
    growth = jnp.exp(scale_field)
    scale_cot = free_part * (coupled_cot * field_in * growth + jac_field)
    net_cot = jnp.concatenate([scale_cot * (1.0 - scale_field * scale_field), free_part * coupled_cot], axis=0).astype(jnp.bfloat16)
    net_cot_f = net_cot.astype(jnp.float32)
    grad_k2 = grads_ref(net_cot_f, hidden_f)
    grad_b2 = lax.optimization_barrier(jnp.sum(net_cot_f, axis=(1, 2, 3, 4)))
    hidden_cot = conv_ref(net_cot_f, kern2[::-1].transpose(0, 2, 1))
    pre_cot = (hidden_cot * (1.0 - hidden_f * hidden_f)).astype(jnp.bfloat16)
    pre_cot_f = pre_cot.astype(jnp.float32)
    grad_k1 = grads_ref(pre_cot_f, frozen_f)
    grad_b1 = lax.optimization_barrier(jnp.sum(pre_cot_f, axis=(1, 2, 3, 4)))
    frozen_cot = conv_ref(pre_cot_f, kern1[::-1].transpose(0, 2, 1))
    field_cot = keep * (coupled_cot + frozen_cot) + free_part * coupled_cot * growth
    norm = 1.0 / math.sqrt(SITES_ALL)
    mix_grad = norm * mix_sum
    lower_full = jnp.dot(jnp.dot(permuter.T, mix_grad, precision=HIGH), upper_tri.T, precision=HIGH)
    upper_full = jnp.dot(lower_tri.T, jnp.dot(permuter.T, mix_grad, precision=HIGH), precision=HIGH)
    grad_lower = jnp.tril(lower_full, -1)
    grad_upper = jnp.triu(upper_full, 1)
    grad_logs = jnp.diagonal(upper_full) * jnp.exp(log_scale) + norm * jnp.sum(jac_cot)
    return (field_in.reshape(chans, slices, -1), field_cot.reshape(chans, slices, -1), norm * grad_k1, norm * grad_b1, norm * grad_k2, norm * grad_b2, grad_lower, grad_upper, grad_logs)
```

```python
import functools
import math

import jax
import jax.numpy as jnp
from jax import lax
from jax.experimental import pallas as pl
from jax.experimental.pallas import tpu as pltpu
from jax.sharding import PartitionSpec as P

LX = 8
LY = 8
LZ = 16
ROW = LY * LZ

HIGH = lax.Precision.HIGHEST
F32 = jnp.float32
BF16 = jnp.bfloat16
VMEM_LIMIT = 48 * 1024 * 1024


def dot(a, b, precision=None):
    return lax.dot_general(
        a, b, (((1,), (0,)), ((), ())), precision=precision, preferred_element_type=F32
    )


def dot_tn(a, b, precision=None):
    return lax.dot_general(
        a, b, (((0,), (0,)), ((), ())), precision=precision, preferred_element_type=F32
    )


def dot_nt(a, b, precision=None):
    return lax.dot_general(
        a, b, (((1,), (1,)), ((), ())), precision=precision, preferred_element_type=F32
    )


def iota(shape, dim):
    return lax.broadcasted_iota(jnp.int32, shape, dim)


def column(row):
    count = row.shape[1]
    same = iota((count, count), 0) == iota((count, count), 1)
    return jnp.sum(jnp.where(same, row, 0.0), axis=1, keepdims=True)


def nilpotent_inverse(nilpart):
    count = nilpart.shape[0]
    eye = jnp.where(iota((count, count), 0) == iota((count, count), 1), 1.0, 0.0)
    result = eye - nilpart
    power = dot(nilpart, nilpart, HIGH)
    span = 2
    while span < count:
        result = dot(result, eye + power, HIGH)
        power = dot(power, power, HIGH)
        span = span * 2
    return result


def factors(perm_row, lower_param, upper_param, log_row):
    chans = lower_param.shape[0]
    rows, cols = iota((chans, chans), 0), iota((chans, chans), 1)
    strict_low = jnp.where(rows > cols, lower_param, 0.0)
    strict_up = jnp.where(cols > rows, upper_param, 0.0)
    diag = column(jnp.exp(log_row))
    perm_t = jnp.where(rows == perm_row, 1.0, 0.0)
    lower_tri = strict_low + jnp.where(rows == cols, 1.0, 0.0)
    upper_tri = strict_up + jnp.where(rows == cols, diag, 0.0)
    return strict_low, strict_up, lower_tri, upper_tri, perm_t, diag


def to_tiles(v):
    return jnp.concatenate([v[:, x * ROW : (x + 1) * ROW] for x in range(LX)], axis=0)


def to_lanes(v):
    chans = v.shape[0] // LX
    return jnp.concatenate([v[x * chans : (x + 1) * chans] for x in range(LX)], axis=1)


def shift_z(v, off):
    if off == 0:
        return v
    z = iota(v.shape, 1) % LZ
    if off > 0:
        return jnp.where(z == LZ - 1, pltpu.roll(v, LZ - 1, 1), pltpu.roll(v, ROW - 1, 1))
    return jnp.where(z == 0, pltpu.roll(v, ROW - LZ + 1, 1), pltpu.roll(v, 1, 1))


def shift_y(v, off):
    if off == 0:
        return v
    return pltpu.roll(v, (ROW - off * LZ) % ROW, 1)


def shift_x(v, off):
    if off == 0:
        return v
    if off > 0:
        return jnp.concatenate([v[:, ROW:], v[:, :ROW]], axis=1)
    return jnp.concatenate([v[:, -ROW:], v[:, :-ROW]], axis=1)


def store_plane_stack(ref, slot, v):
    chans = v.shape[0]
    tiles = to_tiles(v)
    along_z = [shift_z(tiles, e) for e in (-1, 0, 1)]
    for c in (-1, 0, 1):
        for e in (-1, 0, 1):
            k = 3 * (c + 1) + e + 1
            piece = to_lanes(shift_y(along_z[e + 1], c)).astype(BF16)
            ref[slot, k * chans : (k + 1) * chans, :] = piece


def unstack_plane(q):
    chans = q.shape[0] // 9
    total = None
    for e in (-1, 0, 1):
        along = None
        for c in (-1, 0, 1):
            k = 3 * (c + 1) + e + 1
            piece = shift_y(to_tiles(q[k * chans : (k + 1) * chans]), -c)
            along = piece if along is None else along + piece
        along = shift_z(along, -e)
        total = along if total is None else total + along
    return to_lanes(total)


def valid_taps(source, count):
    taps = [a for a in (-1, 0, 1) if 0 <= source - a < count]
    return taps[0], taps[-1] + 1


def add_forward(outs, weight, stack, source):
    first, end = valid_taps(source, len(outs))
    hid = weight.shape[0] // 9
    prod = dot(weight[3 * hid * (first + 1) : 3 * hid * (end + 1), :], stack)
    for a in range(first, end):
        for b in (-1, 0, 1):
            lo = (3 * (a - first) + b + 1) * hid
            piece = shift_x(prod[lo : lo + hid], b)
            t = source - a
            outs[t] = piece if outs[t] is None else outs[t] + piece


def spread_stack(slices, taps):
    return jnp.concatenate(
        [shift_x(slices[i], -b) for i in range(len(taps)) for b in (-1, 0, 1)], axis=0
    )


def kernel_grads(cot, stacks, count):
    blocks = {}
    for source in range(-1, count + 1):
        first, end = valid_taps(source, count)
        taps = list(range(first, end))
        left = spread_stack([cot[source - a] for a in taps], taps)
        prod = dot_nt(left, stacks(source))
        for i, a in enumerate(taps):
            size = left.shape[0] // len(taps)
            part = prod[i * size : (i + 1) * size]
            blocks[a] = part if a not in blocks else blocks[a] + part
    return jnp.concatenate([blocks[a] for a in (-1, 0, 1)], axis=0)


def to_blocks(grad, fold):
    rows, cols = grad.shape
    full = cols // 128
    rest = cols - full * 128
    parts = [grad[:, i * 128 : (i + 1) * 128] for i in range(full)]
    tail = grad[:, full * 128 :]
    each = rows // fold
    tails = [tail[i * each : (i + 1) * each] for i in range(fold)]
    tails.append(jnp.zeros((each, 128 - rest * fold), F32))
    parts.append(jnp.concatenate(tails, axis=1))
    return jnp.concatenate(parts, axis=0)


def from_blocks(packed, rows, cols, fold):
    full = cols // 128
    rest = cols - full * 128
    each = rows // fold
    parts = [packed[i * rows : (i + 1) * rows] for i in range(full)]
    last = packed[full * rows : full * rows + each]
    tail = jnp.concatenate([last[:, i * rest : (i + 1) * rest] for i in range(fold)], axis=0)
    return jnp.concatenate(parts + [tail], axis=1)


def block_rows(rows, cols, fold, n):
    total = (cols // 128) * rows + rows // fold
    blocks = -(-total // 16)
    return total, 16 * -(-blocks // n)


FOLD1 = 3
FOLD2 = 1


def main_kernel(
    n,
    out_field,
    out_cot,
    jac,
    mask,
    perm,
    lower,
    upper,
    logs,
    kern1,
    bias1,
    kern2,
    bias2,
    field_in_o,
    field_cot_o,
    gath1_o,
    gath2_o,
    small_o,
    frozen,
    stack1,
    stack2,
    ncot,
    pcot,
    w1,
    w1t,
    w2,
    w2t,
    send1,
    recv1,
    gath1,
    send2,
    recv2,
    gath2,
    small_mine,
    small_all,
    halo_send,
    halo_recv,
    s1_send,
    s1_recv,
    s2_send,
    s2_recv,
    g1_send,
    g1_recv,
    g2_send,
    g2_recv,
    sm_send,
    sm_recv,
):
    me = lax.axis_index("ta")
    chans, count, sites = out_field.shape
    hid = kern1.shape[2]
    right, left = lax.rem(me + 1, n), lax.rem(me + n - 1, n)

    barrier = pltpu.get_barrier_semaphore()

    def greet(k, carry):
        pl.semaphore_signal(barrier, inc=1, device_id={"ta": lax.rem(me + k, n)})
        return carry

    lax.fori_loop(1, n, greet, 0)

    strict_low, strict_up, lower_tri, upper_tri, perm_t, diag = factors(
        perm[...], lower[...], upper[...], logs[...]
    )
    inv_diag_row = jnp.exp(logs[...])
    upper_inv = nilpotent_inverse(strict_up / diag) * (1.0 / inv_diag_row)
    lower_inv = nilpotent_inverse(strict_low)
    unmixer = dot(dot(upper_inv, lower_inv, HIGH), perm_t, HIGH)
    mixer = dot_tn(perm_t, dot(lower_tri, upper_tri, HIGH), HIGH)

    keep = [mask[t : t + 1, :].astype(F32) for t in range(count)]
    coupled = [dot(unmixer, out_field[:, t, :], HIGH) for t in range(count)]
    for t in range(count):
        frozen[2 + t] = (keep[t] * coupled[t]).astype(BF16)

    pl.semaphore_wait(barrier, n - 1)

    def halo(index, src, dst, where):
        return pltpu.make_async_remote_copy(
            src_ref=src,
            dst_ref=dst,
            send_sem=halo_send.at[index],
            recv_sem=halo_recv.at[index],
            device_id={"ta": where},
        )

    def exchange(base, buf, width):
        up = halo(base, buf.at[pl.ds(count, width)], buf.at[pl.ds(0, width)], right)
        down = halo(
            base + 1, buf.at[pl.ds(width, width)], buf.at[pl.ds(width + count, width)], left
        )
        up.start()
        down.start()
        return up, down

    first_halo = exchange(0, frozen, 2)

    def spread(send, recv, s_sem, r_sem):
        def step(k, carry):
            peer = lax.rem(me + k, n)
            pltpu.make_async_remote_copy(
                src_ref=send.at[peer],
                dst_ref=recv.at[k],
                send_sem=s_sem.at[k],
                recv_sem=r_sem.at[k],
                device_id={"ta": peer},
            ).start()
            return carry

        lax.fori_loop(1, n, step, 0)

    def collect(send, recv, s_sem, r_sem):
        def step(k, total):
            peer = lax.rem(me + k, n)
            pltpu.make_async_remote_copy(
                src_ref=send.at[peer],
                dst_ref=recv.at[k],
                send_sem=s_sem.at[k],
                recv_sem=r_sem.at[k],
                device_id={"ta": peer},
            ).wait()
            return total + recv[k].astype(F32)

        return lax.fori_loop(1, n, step, send[me].astype(F32))

    def share(buf, s_sem, r_sem):
        def step(k, carry):
            pltpu.make_async_remote_copy(
                src_ref=buf.at[me],
                dst_ref=buf.at[me],
                send_sem=s_sem.at[k],
                recv_sem=r_sem.at[k],
                device_id={"ta": lax.rem(me + k, n)},
            ).start()
            return carry

        lax.fori_loop(1, n, step, 0)

    def share_done(buf, s_sem, r_sem):
        def step(k, carry):
            peer = lax.rem(me + n - k, n)
            done = pltpu.make_async_remote_copy(
                src_ref=buf.at[me],
                dst_ref=buf.at[peer],
                send_sem=s_sem.at[k],
                recv_sem=r_sem.at[k],
                device_id={"ta": lax.rem(me + k, n)},
            )
            done.wait_recv()
            done.wait_send()
            return carry

        lax.fori_loop(1, n, step, 0)

    for kern, w, wt in ((kern1, w1, w1t), (kern2, w2, w2t)):
        ins = kern.shape[3]
        wide = jnp.concatenate(
            [kern[:, k].astype(F32).reshape(9 * hid, ins) for k in range(9)], axis=1
        )
        w[...] = wide.astype(BF16)
        wt[...] = wide.T.astype(BF16)

    coupled_cot = [dot_tn(mixer, out_cot[:, t, :], HIGH) for t in range(count)]
    mix = None
    for t in range(count):
        term = dot_nt(out_cot[:, t, :], coupled[t], HIGH)
        mix = term if mix is None else mix + term
    jac_sum = jnp.sum(jnp.sum(jac[...], axis=1, keepdims=True), axis=0, keepdims=True)

    hidden_pre = [None] * (count + 2)
    for slot in range(2, count + 2):
        store_plane_stack(stack1, slot, frozen[slot].astype(F32))
        add_forward(hidden_pre, w1, stack1[slot], slot - 1)
    for copy in first_halo:
        copy.wait()
    for slot in [0, 1] + [count + 2, count + 3]:
        store_plane_stack(stack1, slot, frozen[slot].astype(F32))
        add_forward(hidden_pre, w1, stack1[slot], slot - 1)

    bias1_col = column(bias1[...])
    bias2_col = column(bias2[...])
    net = [None] * count
    hidden_mid = []
    for slot in range(count + 2):
        hidden = jnp.tanh(hidden_pre[slot] + bias1_col).astype(BF16).astype(F32)
        if 1 <= slot <= count:
            hidden_mid.append(hidden)
        store_plane_stack(stack2, slot, hidden)
        add_forward(net, w2, stack2[slot], slot - 1)

    growth = []
    cots = []
    for t in range(count):
        net_t = net[t] + bias2_col
        scale = jnp.tanh(net_t[:chans])
        shift = net_t[chans:]
        free = 1.0 - keep[t]
        grow = jnp.exp(scale)
        growth.append(grow)
        fin = keep[t] * coupled[t] + free * (coupled[t] - shift) * jnp.exp(-scale)
        field_in_o[:, t, :] = fin
        scale_cot = free * (coupled_cot[t] * fin * grow + jac[t : t + 1, :])
        cot = jnp.concatenate(
            [scale_cot * (1.0 - scale * scale), free * coupled_cot[t]], axis=0
        ).astype(BF16)
        ncot[1 + t] = cot
        cots.append(cot)
    second_halo = exchange(2, ncot, 1)

    grads2 = kernel_grads(cots, lambda s: stack2[s + 1], count)
    total2, rows2 = block_rows(9 * hid, 9 * hid, FOLD2, n)
    packed2 = to_blocks(grads2, FOLD2)
    packed2 = jnp.concatenate(
        [packed2, jnp.zeros((n * rows2 - total2, 128), F32)], axis=0
    ).astype(BF16)
    for p in range(n):
        send2[p] = packed2[p * rows2 : (p + 1) * rows2]
    spread(send2, recv2, s2_send, s2_recv)

    ones = jnp.ones((8, sites), BF16)
    bias2_row = sum(dot_nt(ones, c) for c in cots)

    for copy in second_halo:
        copy.wait()
    pres = []
    for t in range(count):
        taps = (-1, 0, 1)
        wide = spread_stack([ncot[1 + t - a] for a in taps], taps)
        hidden_cot = unstack_plane(dot(w2t[...], wide))
        pre = (hidden_cot * (1.0 - hidden_mid[t] * hidden_mid[t])).astype(BF16)
        pcot[1 + t] = pre
        pres.append(pre)
    third_halo = exchange(4, pcot, 1)

    grads1 = kernel_grads(pres, lambda s: stack1[s + 2], count)
    total1, rows1 = block_rows(9 * hid, 9 * chans, FOLD1, n)
    packed1 = to_blocks(grads1, FOLD1)
    packed1 = jnp.concatenate(
        [packed1, jnp.zeros((n * rows1 - total1, 128), F32)], axis=0
    ).astype(BF16)
    for p in range(n):
        send1[p] = packed1[p * rows1 : (p + 1) * rows1]
    spread(send1, recv1, s1_send, s1_recv)

    bias1_row = sum(dot_nt(ones, c) for c in pres)
    small_mine[...] = jnp.concatenate(
        [mix[:8], mix[8:], bias1_row, bias2_row, jnp.broadcast_to(jac_sum, (8, 32))], axis=1
    )

    def small_copy(k):
        return pltpu.make_async_remote_copy(
            src_ref=small_mine,
            dst_ref=small_all.at[k],
            send_sem=sm_send.at[k],
            recv_sem=sm_recv.at[k],
            device_id={"ta": lax.rem(me + k, n)},
        )

    def small_start(k, carry):
        small_copy(k).start()
        return carry

    lax.fori_loop(1, n, small_start, 0)

    gath2[me] = collect(send2, recv2, s2_send, s2_recv).astype(BF16)
    share(gath2, g2_send, g2_recv)

    for copy in third_halo:
        copy.wait()
    for t in range(count):
        taps = (-1, 0, 1)
        wide = spread_stack([pcot[1 + t - a] for a in taps], taps)
        frozen_cot = unstack_plane(dot(w1t[...], wide))
        free = 1.0 - keep[t]
        field_cot_o[:, t, :] = (
            keep[t] * (coupled_cot[t] + frozen_cot) + free * coupled_cot[t] * growth[t]
        )

    gath1[me] = collect(send1, recv1, s1_send, s1_recv).astype(BF16)
    share(gath1, g1_send, g1_recv)

    def small_done(k, carry):
        small_copy(k).wait()
        return carry

    lax.fori_loop(1, n, small_done, 0)
    small_all[0] = small_mine[...]

    def small_add(k, total):
        return total + small_all[lax.rem(me + n - k, n)]

    small_o[...] = lax.fori_loop(0, n, small_add, jnp.zeros(small_mine.shape, F32))

    share_done(gath2, g2_send, g2_recv)
    gath2_o[...] = gath2[...]
    share_done(gath1, g1_send, g1_recv)
    gath1_o[...] = gath1[...]


def last_kernel(
    norm,
    field_in,
    field_cot,
    gath1,
    gath2,
    small,
    perm,
    lower,
    upper,
    logs,
    field_in_o,
    field_cot_o,
    kern1_o,
    bias1_o,
    kern2_o,
    bias2_o,
    lower_o,
    upper_o,
    logs_o,
):
    field_in_o[...] = field_in[...]
    field_cot_o[...] = field_cot[...]
    for gath, out, fold in ((gath1, kern1_o, FOLD1), (gath2, kern2_o, FOLD2)):
        hid, ins = out.shape[2], out.shape[3]
        grid = from_blocks(gath[...].astype(F32) * norm, 9 * hid, 9 * ins, fold)
        for k in range(9):
            out[:, k] = grid[:, k * ins : (k + 1) * ins].reshape(9, hid, ins)
    _, _, lower_tri, upper_tri, perm_t, _ = factors(
        perm[...], lower[...], upper[...], logs[...]
    )
    sums = small[...] * norm
    chans = lower.shape[0]
    hid = bias1_o.shape[1]
    mix = jnp.concatenate([sums[:, :chans], sums[:, chans : 2 * chans]], axis=0)
    base = 2 * chans
    bias1_o[...] = sums[0:1, base : base + hid]
    bias2_o[...] = sums[0:1, base + hid : base + 2 * hid]
    turned = dot(perm_t, mix, HIGH)
    lower_full = dot_nt(turned, upper_tri, HIGH)
    upper_full = dot_tn(lower_tri, turned, HIGH)
    rows, cols = iota((chans, chans), 0), iota((chans, chans), 1)
    lower_o[...] = jnp.where(rows > cols, lower_full, 0.0)
    upper_o[...] = jnp.where(cols > rows, upper_full, 0.0)
    diag = jnp.sum(jnp.where(rows == cols, upper_full, 0.0), axis=0, keepdims=True)
    jac_row = sums[0:1, base + 2 * hid : base + 2 * hid + chans]
    logs_o[...] = diag * jnp.exp(logs[...]) + jac_row


def body(
    n,
    out_field,
    out_cot,
    jac_cot,
    mask,
    perm,
    lower_param,
    upper_param,
    log_scale,
    kern1,
    bias1,
    kern2,
    bias2,
):
    chans, count, sites = out_field.shape
    hid = kern1.shape[1]
    perm_row = perm.reshape(1, chans)
    log_row = log_scale.reshape(1, chans)
    _, rows1 = block_rows(9 * hid, 9 * chans, FOLD1, n)
    _, rows2 = block_rows(9 * hid, 9 * hid, FOLD2, n)
    vmem = pl.BlockSpec(memory_space=pltpu.VMEM)
    shape = jax.ShapeDtypeStruct
    field = shape((chans, count, sites), F32)
    dma = pltpu.SemaphoreType.DMA
    field_in, field_cot, gath1, gath2, small = pl.pallas_call(
        functools.partial(main_kernel, n),
        out_shape=(
            field,
            field,
            shape((n, rows1, 128), BF16),
            shape((n, rows2, 128), BF16),
            shape((8, 128), F32),
        ),
        in_specs=[vmem] * 12,
        out_specs=(vmem,) * 5,
        scratch_shapes=[
            pltpu.VMEM((count + 4, chans, sites), BF16),
            pltpu.VMEM((count + 4, 9 * chans, sites), BF16),
            pltpu.VMEM((count + 2, 9 * hid, sites), BF16),
            pltpu.VMEM((count + 2, hid, sites), BF16),
            pltpu.VMEM((count + 2, hid, sites), BF16),
            pltpu.VMEM((9 * hid, 9 * chans), BF16),
            pltpu.VMEM((9 * chans, 9 * hid), BF16),
            pltpu.VMEM((9 * hid, 9 * hid), BF16),
            pltpu.VMEM((9 * hid, 9 * hid), BF16),
        ]
        + [pltpu.VMEM((n, rows1, 128), BF16)] * 3
        + [pltpu.VMEM((n, rows2, 128), BF16)] * 3
        + [pltpu.VMEM((8, 128), F32), pltpu.VMEM((n, 8, 128), F32)]
        + [dma((6,))] * 2
        + [dma((n,))] * 10,
        compiler_params=pltpu.CompilerParams(
            collective_id=0, has_side_effects=True, vmem_limit_bytes=VMEM_LIMIT
        ),
        name="block_backward",
    )(
        out_field,
        out_cot,
        jac_cot,
        mask,
        perm_row,
        lower_param,
        upper_param,
        log_row,
        kern1.reshape(9, 9, hid, chans),
        bias1.reshape(1, hid),
        kern2.reshape(9, 9, kern2.shape[1], hid),
        bias2.reshape(1, -1),
    )
    norm = 1.0 / math.sqrt(count * sites * n)
    outs = pl.pallas_call(
        functools.partial(last_kernel, norm),
        out_shape=(
            field,
            field,
            shape((9, 9, hid, chans), F32),
            shape((1, hid), F32),
            shape((9, 9, 2 * chans, hid), F32),
            shape((1, 2 * chans), F32),
            shape((chans, chans), F32),
            shape((chans, chans), F32),
            shape((1, chans), F32),
        ),
        in_specs=[vmem] * 9,
        out_specs=(vmem,) * 9,
        compiler_params=pltpu.CompilerParams(vmem_limit_bytes=VMEM_LIMIT),
        name="unpack",
    )(
        field_in,
        field_cot,
        gath1.reshape(n * rows1, 128),
        gath2.reshape(n * rows2, 128),
        small,
        perm_row,
        lower_param,
        upper_param,
        log_row,
    )
    return (
        outs[0],
        outs[1],
        outs[2].reshape(81, hid, chans),
        outs[3].reshape(-1),
        outs[4].reshape(81, 2 * chans, hid),
        outs[5].reshape(-1),
        outs[6],
        outs[7],
        outs[8].reshape(-1),
    )


def solution(mesh):
    split = ("groups", "ta")
    in_specs = (
        P(None, split, None),
        P(None, split, None),
        P(split, None),
        P(split, None),
    ) + (P(),) * 8
    out_specs = (
        P(None, split, None),
        P(None, split, None),
        P("groups", None, None),
        P("groups"),
        P("groups", None, None),
        P("groups"),
        P("groups", None),
        P("groups", None),
        P("groups"),
    )
    return jax.shard_map(
        functools.partial(body, mesh.shape["ta"]),
        mesh=mesh,
        in_specs=in_specs,
        out_specs=out_specs,
        check_vma=False,
    )
```

```python
import functools
import math

import jax
import jax.numpy as jnp
from jax import lax
from jax.experimental import pallas as pl
from jax.experimental.pallas import tpu as pltpu
from jax.sharding import PartitionSpec as P

LX = 8
LY = 8
LZ = 16
ROW = LY * LZ

HIGH = lax.Precision.HIGHEST
F32 = jnp.float32
BF16 = jnp.bfloat16
VMEM_LIMIT = 48 * 1024 * 1024


def dot(a, b, precision=None):
    return lax.dot_general(
        a, b, (((1,), (0,)), ((), ())), precision=precision, preferred_element_type=F32
    )


def dot_tn(a, b, precision=None):
    return lax.dot_general(
        a, b, (((0,), (0,)), ((), ())), precision=precision, preferred_element_type=F32
    )


def dot_nt(a, b, precision=None):
    return lax.dot_general(
        a, b, (((1,), (1,)), ((), ())), precision=precision, preferred_element_type=F32
    )


def split3(v):
    first = v.astype(BF16)
    rest = v - first.astype(F32)
    second = rest.astype(BF16)
    return first, second, (rest - second.astype(F32)).astype(BF16)


def mix_field(matrix, pieces):
    m1, m2, m3 = (m.astype(F32) for m in split3(matrix))
    x1, x2, x3 = pieces
    left = jnp.concatenate([m1, m1, m1, m2, m2, m3], axis=1).astype(BF16)
    return dot(left, jnp.concatenate([x1, x2, x3, x1, x2, x1], axis=0))


def iota(shape, dim):
    return lax.broadcasted_iota(jnp.int32, shape, dim)


def column(row):
    count = row.shape[1]
    same = iota((count, count), 0) == iota((count, count), 1)
    return jnp.sum(jnp.where(same, row, 0.0), axis=1, keepdims=True)


def nilpotent_inverse(nilpart):
    count = nilpart.shape[0]
    eye = jnp.where(iota((count, count), 0) == iota((count, count), 1), 1.0, 0.0)
    result = eye - nilpart
    power = dot(nilpart, nilpart, HIGH)
    span = 2
    while span < count:
        result = dot(result, eye + power, HIGH)
        power = dot(power, power, HIGH)
        span = span * 2
    return result


def factors(perm_row, lower_param, upper_param, log_row):
    chans = lower_param.shape[0]
    rows, cols = iota((chans, chans), 0), iota((chans, chans), 1)
    strict_low = jnp.where(rows > cols, lower_param, 0.0)
    strict_up = jnp.where(cols > rows, upper_param, 0.0)
    diag = column(jnp.exp(log_row))
    perm_t = jnp.where(rows == perm_row, 1.0, 0.0)
    lower_tri = strict_low + jnp.where(rows == cols, 1.0, 0.0)
    upper_tri = strict_up + jnp.where(rows == cols, diag, 0.0)
    return strict_low, strict_up, lower_tri, upper_tri, perm_t, diag


def to_tiles(v):
    return jnp.concatenate([v[:, x * ROW : (x + 1) * ROW] for x in range(LX)], axis=0)


def to_lanes(v):
    chans = v.shape[0] // LX
    return jnp.concatenate([v[x * chans : (x + 1) * chans] for x in range(LX)], axis=1)


def shift_z(v, off):
    if off == 0:
        return v
    z = iota(v.shape, 1) % LZ
    if off > 0:
        return jnp.where(z == LZ - 1, pltpu.roll(v, LZ - 1, 1), pltpu.roll(v, ROW - 1, 1))
    return jnp.where(z == 0, pltpu.roll(v, ROW - LZ + 1, 1), pltpu.roll(v, 1, 1))


def shift_y(v, off):
    if off == 0:
        return v
    return pltpu.roll(v, (ROW - off * LZ) % ROW, 1)


def shift_x(v, off):
    if off == 0:
        return v
    if off > 0:
        return jnp.concatenate([v[:, ROW:], v[:, :ROW]], axis=1)
    return jnp.concatenate([v[:, -ROW:], v[:, :-ROW]], axis=1)


def store_plane_stack(ref, slot, v):
    chans = v.shape[0]
    tiles = to_tiles(v)
    along_z = [shift_z(tiles, e) for e in (-1, 0, 1)]
    for c in (-1, 0, 1):
        for e in (-1, 0, 1):
            k = 3 * (c + 1) + e + 1
            piece = to_lanes(shift_y(along_z[e + 1], c)).astype(BF16)
            ref[slot, k * chans : (k + 1) * chans, :] = piece


def unstack_plane(q):
    chans = q.shape[0] // 9
    total = None
    for e in (-1, 0, 1):
        along = None
        for c in (-1, 0, 1):
            k = 3 * (c + 1) + e + 1
            piece = shift_y(to_tiles(q[k * chans : (k + 1) * chans]), -c)
            along = piece if along is None else along + piece
        along = shift_z(along, -e)
        total = along if total is None else total + along
    return to_lanes(total)


def valid_taps(source, count):
    taps = [a for a in (-1, 0, 1) if 0 <= source - a < count]
    return taps[0], taps[-1] + 1


def add_forward(outs, weight, stack, source):
    first, end = valid_taps(source, len(outs))
    hid = weight.shape[0] // 9
    prod = dot(weight[3 * hid * (first + 1) : 3 * hid * (end + 1), :], stack)
    for a in range(first, end):
        for b in (-1, 0, 1):
            lo = (3 * (a - first) + b + 1) * hid
            piece = shift_x(prod[lo : lo + hid], b)
            t = source - a
            outs[t] = piece if outs[t] is None else outs[t] + piece


def spread_stack(slices, taps):
    return jnp.concatenate(
        [shift_x(slices[i], -b) for i in range(len(taps)) for b in (-1, 0, 1)], axis=0
    )


def kernel_grads(cot, stacks, count):
    blocks = {}
    for source in range(-1, count + 1):
        first, end = valid_taps(source, count)
        taps = list(range(first, end))
        left = spread_stack([cot[source - a] for a in taps], taps)
        prod = dot_nt(left, stacks(source))
        for i, a in enumerate(taps):
            size = left.shape[0] // len(taps)
            part = prod[i * size : (i + 1) * size]
            blocks[a] = part if a not in blocks else blocks[a] + part
    return jnp.concatenate([blocks[a] for a in (-1, 0, 1)], axis=0)


def to_blocks(grad, fold):
    rows, cols = grad.shape
    full = cols // 128
    rest = cols - full * 128
    parts = [grad[:, i * 128 : (i + 1) * 128] for i in range(full)]
    tail = grad[:, full * 128 :]
    each = rows // fold
    tails = [tail[i * each : (i + 1) * each] for i in range(fold)]
    tails.append(jnp.zeros((each, 128 - rest * fold), F32))
    parts.append(jnp.concatenate(tails, axis=1))
    return jnp.concatenate(parts, axis=0)


def from_blocks(packed, rows, cols, fold):
    full = cols // 128
    rest = cols - full * 128
    each = rows // fold
    parts = [packed[i * rows : (i + 1) * rows] for i in range(full)]
    last = packed[full * rows : full * rows + each]
    tail = jnp.concatenate([last[:, i * rest : (i + 1) * rest] for i in range(fold)], axis=0)
    return jnp.concatenate(parts + [tail], axis=1)


def block_rows(rows, cols, fold, n):
    total = (cols // 128) * rows + rows // fold
    blocks = -(-total // 16)
    return total, 16 * -(-blocks // n)


FOLD1 = 3
FOLD2 = 1


def main_kernel(
    n,
    out_field,
    out_cot,
    jac,
    mask,
    perm,
    lower,
    upper,
    logs,
    kern1,
    bias1,
    kern2,
    bias2,
    field_in_o,
    field_cot_o,
    gath1_o,
    gath2_o,
    small_o,
    frozen,
    stack1,
    stack2,
    ncot,
    pcot,
    w1,
    w1t,
    w2,
    w2t,
    send1,
    gath1,
    paired1,
    recv1,
    send2,
    gath2,
    paired2,
    recv2,
    small_mine,
    small_other,
    small_all,
    p1_sem,
    p2_sem,
    ps_sem,
    halo_send,
    halo_recv,
    s1_send,
    s1_recv,
    s2_send,
    s2_recv,
    g1_send,
    g1_recv,
    g2_send,
    g2_recv,
    sm_send,
    sm_recv,
    f1_send,
    f1_recv,
    f2_send,
    f2_recv,
):
    me = lax.axis_index("ta")
    chans, count, sites = out_field.shape
    hid = kern1.shape[2]
    right, left = lax.rem(me + 1, n), lax.rem(me + n - 1, n)
    chips = n // 2
    chip, core = me // 2, lax.rem(me, 2)
    other = 1 - core
    partner = 2 * chip + other

    barrier = pltpu.get_barrier_semaphore()

    def greet(k, carry):
        pl.semaphore_signal(barrier, inc=1, device_id={"ta": lax.rem(me + k, n)})
        return carry

    lax.fori_loop(1, n, greet, 0)

    strict_low, strict_up, lower_tri, upper_tri, perm_t, diag = factors(
        perm[...], lower[...], upper[...], logs[...]
    )
    inv_diag_row = jnp.exp(logs[...])
    upper_inv = nilpotent_inverse(strict_up / diag) * (1.0 / inv_diag_row)
    lower_inv = nilpotent_inverse(strict_low)
    unmixer = dot(dot(upper_inv, lower_inv, HIGH), perm_t, HIGH)
    mixer_t = dot_tn(dot(lower_tri, upper_tri, HIGH), perm_t, HIGH)

    keep = [mask[t : t + 1, :].astype(F32) for t in range(count)]
    coupled = [mix_field(unmixer, split3(out_field[:, t, :])) for t in range(count)]
    for t in range(count):
        frozen[2 + t] = (keep[t] * coupled[t]).astype(BF16)

    pl.semaphore_wait(barrier, n - 1)

    def halo(index, src, dst, where):
        return pltpu.make_async_remote_copy(
            src_ref=src,
            dst_ref=dst,
            send_sem=halo_send.at[index],
            recv_sem=halo_recv.at[index],
            device_id={"ta": where},
        )

    def exchange(base, buf, width):
        up = halo(base, buf.at[pl.ds(count, width)], buf.at[pl.ds(0, width)], right)
        down = halo(
            base + 1, buf.at[pl.ds(width, width)], buf.at[pl.ds(width + count, width)], left
        )
        up.start()
        down.start()
        return up, down

    first_halo = exchange(0, frozen, 2)

    def remote(src, dst, send_sem, recv_sem, where):
        return pltpu.make_async_remote_copy(
            src_ref=src,
            dst_ref=dst,
            send_sem=send_sem,
            recv_sem=recv_sem,
            device_id={"ta": where},
        )

    def ahead(k):
        return lax.rem(chip + k, chips)

    def behind(k):
        return lax.rem(chip + chips - k, chips)

    def each(step):
        def run(k, carry):
            step(k)
            return carry

        lax.fori_loop(1, chips, run, 0)

    def pair_copy(send, paired, sems):
        return remote(send.at[other], paired, sems.at[0], sems.at[1], partner)

    def load_send(send, packed):
        rows = send.shape[2]
        for p in range(n):
            send[p // chips, p % chips] = packed[p * rows : (p + 1) * rows]

    def pair_sum(send, paired):
        paired[...] = (send[core].astype(F32) + paired[...].astype(F32)).astype(BF16)

    def scatter_copy(paired, recv, s_sem, r_sem, k):
        return remote(
            paired.at[ahead(k)], recv.at[k], s_sem.at[k], r_sem.at[k], 2 * ahead(k) + core
        )

    def scatter(*refs):
        each(lambda k: scatter_copy(*refs, k).start())

    def collect(paired, recv, s_sem, r_sem):
        def step(k, total):
            scatter_copy(paired, recv, s_sem, r_sem, k).wait()
            return total + recv[k].astype(F32)

        return lax.fori_loop(1, chips, step, paired[chip].astype(F32)).astype(BF16)

    def gather_copy(buf, s_sem, r_sem, k, at):
        return remote(
            buf.at[core, chip], buf.at[core, at], s_sem.at[k], r_sem.at[k], 2 * ahead(k) + core
        )

    def forward_copy(buf, f_send, f_recv, k, to):
        return remote(
            buf.at[core, behind(k)], buf.at[to, behind(k)], f_send.at[k], f_recv.at[k], partner
        )

    def gather(buf, s_sem, r_sem, f_send, f_recv):
        forward_copy(buf, f_send, f_recv, 0, core).start()
        each(lambda k: gather_copy(buf, s_sem, r_sem, k, chip).start())

    def gather_forward(buf, s_sem, r_sem, f_send, f_recv):
        def step(k):
            gather_copy(buf, s_sem, r_sem, k, behind(k)).wait_recv()
            forward_copy(buf, f_send, f_recv, k, core).start()

        each(step)

    def gather_done(buf, s_sem, r_sem, f_send, f_recv):
        def step(k):
            gather_copy(buf, s_sem, r_sem, k, chip).wait_send()
            forward_copy(buf, f_send, f_recv, k, core).wait_send()
            forward_copy(buf, f_send, f_recv, k, other).wait_recv()

        forward_copy(buf, f_send, f_recv, 0, core).wait_send()
        forward_copy(buf, f_send, f_recv, 0, other).wait_recv()
        each(step)

    for kern, w, wt in ((kern1, w1, w1t), (kern2, w2, w2t)):
        ins = kern.shape[3]
        wide = jnp.concatenate(
            [kern[:, k].astype(F32).reshape(9 * hid, ins) for k in range(9)], axis=1
        )
        w[...] = wide.astype(BF16)
        wt[...] = wide.T.astype(BF16)

    cot_pieces = [split3(out_cot[:, t, :]) for t in range(count)]
    coupled_cot = [mix_field(mixer_t, cot_pieces[t]) for t in range(count)]
    wide_mix = None
    for t in range(count):
        term = dot_nt(
            jnp.concatenate(cot_pieces[t], axis=0),
            jnp.concatenate(split3(coupled[t]), axis=0),
        )
        wide_mix = term if wide_mix is None else wide_mix + term
    mix = None
    for i, j in ((2, 0), (1, 1), (0, 2), (1, 0), (0, 1), (0, 0)):
        term = wide_mix[i * chans : (i + 1) * chans, j * chans : (j + 1) * chans]
        mix = term if mix is None else mix + term
    jac_sum = jnp.sum(jnp.sum(jac[...], axis=1, keepdims=True), axis=0, keepdims=True)

    hidden_pre = [None] * (count + 2)
    for slot in range(2, count + 2):
        store_plane_stack(stack1, slot, frozen[slot].astype(F32))
        add_forward(hidden_pre, w1, stack1[slot], slot - 1)
    for copy in first_halo:
        copy.wait()
    for slot in [0, 1] + [count + 2, count + 3]:
        store_plane_stack(stack1, slot, frozen[slot].astype(F32))
        add_forward(hidden_pre, w1, stack1[slot], slot - 1)

    bias1_col = column(bias1[...])
    bias2_col = column(bias2[...])
    net = [None] * count
    hidden_mid = []
    for slot in range(count + 2):
        hidden = jnp.tanh(hidden_pre[slot] + bias1_col).astype(BF16).astype(F32)
        if 1 <= slot <= count:
            hidden_mid.append(hidden)
        store_plane_stack(stack2, slot, hidden)
        add_forward(net, w2, stack2[slot], slot - 1)

    growth = []
    cots = []
    for t in range(count):
        net_t = net[t] + bias2_col
        scale = jnp.tanh(net_t[:chans])
        shift = net_t[chans:]
        free = 1.0 - keep[t]
        grow = jnp.exp(scale)
        growth.append(grow)
        fin = keep[t] * coupled[t] + free * (coupled[t] - shift) * jnp.exp(-scale)
        field_in_o[:, t, :] = fin
        scale_cot = free * (coupled_cot[t] * fin * grow + jac[t : t + 1, :])
        cot = jnp.concatenate(
            [scale_cot * (1.0 - scale * scale), free * coupled_cot[t]], axis=0
        ).astype(BF16)
        ncot[1 + t] = cot
        cots.append(cot)
    second_halo = exchange(2, ncot, 1)

    grads2 = kernel_grads(cots, lambda s: stack2[s + 1], count)
    total2, rows2 = block_rows(9 * hid, 9 * hid, FOLD2, n)
    packed2 = to_blocks(grads2, FOLD2)
    packed2 = jnp.concatenate(
        [packed2, jnp.zeros((n * rows2 - total2, 128), F32)], axis=0
    ).astype(BF16)
    load_send(send2, packed2)
    pair2 = pair_copy(send2, paired2, p2_sem)
    pair2.start()

    ones = jnp.ones((8, sites), BF16)
    bias2_row = sum(dot_nt(ones, c) for c in cots)

    for copy in second_halo:
        copy.wait()
    pres = []
    for t in range(count):
        taps = (-1, 0, 1)
        wide = spread_stack([ncot[1 + t - a] for a in taps], taps)
        hidden_cot = unstack_plane(dot(w2t[...], wide))
        pre = (hidden_cot * (1.0 - hidden_mid[t] * hidden_mid[t])).astype(BF16)
        pcot[1 + t] = pre
        pres.append(pre)
    third_halo = exchange(4, pcot, 1)

    pair2.wait()
    pair_sum(send2, paired2)
    scatter(paired2, recv2, s2_send, s2_recv)

    grads1 = kernel_grads(pres, lambda s: stack1[s + 2], count)
    total1, rows1 = block_rows(9 * hid, 9 * chans, FOLD1, n)
    packed1 = to_blocks(grads1, FOLD1)
    packed1 = jnp.concatenate(
        [packed1, jnp.zeros((n * rows1 - total1, 128), F32)], axis=0
    ).astype(BF16)
    load_send(send1, packed1)
    pair1 = pair_copy(send1, paired1, p1_sem)
    pair1.start()

    bias1_row = sum(dot_nt(ones, c) for c in pres)
    small_mine[...] = jnp.concatenate(
        [mix[:8], mix[8:], bias1_row, bias2_row, jnp.broadcast_to(jac_sum, (8, 32))], axis=1
    )
    pair_small = remote(small_mine, small_other, ps_sem.at[0], ps_sem.at[1], partner)
    pair_small.start()

    pair1.wait()
    pair_sum(send1, paired1)
    scatter(paired1, recv1, s1_send, s1_recv)
    pair_small.wait()
    small_all[chip] = small_mine[...] + small_other[...]

    def small_copy(k, at):
        return remote(
            small_all.at[chip],
            small_all.at[at],
            sm_send.at[k],
            sm_recv.at[k],
            2 * ahead(k) + core,
        )

    each(lambda k: small_copy(k, chip).start())

    gath2[core, chip] = collect(paired2, recv2, s2_send, s2_recv)
    gather(gath2, g2_send, g2_recv, f2_send, f2_recv)

    for copy in third_halo:
        copy.wait()
    for t in range(count):
        taps = (-1, 0, 1)
        wide = spread_stack([pcot[1 + t - a] for a in taps], taps)
        frozen_cot = unstack_plane(dot(w1t[...], wide))
        free = 1.0 - keep[t]
        field_cot_o[:, t, :] = (
            keep[t] * (coupled_cot[t] + frozen_cot) + free * coupled_cot[t] * growth[t]
        )

    gath1[core, chip] = collect(paired1, recv1, s1_send, s1_recv)
    gather(gath1, g1_send, g1_recv, f1_send, f1_recv)

    gather_forward(gath2, g2_send, g2_recv, f2_send, f2_recv)

    def small_done(k):
        small_copy(k, chip).wait_send()
        small_copy(k, behind(k)).wait_recv()

    each(small_done)
    small_o[...] = lax.fori_loop(
        0, chips, lambda k, total: total + small_all[k], jnp.zeros(small_mine.shape, F32)
    )

    gather_forward(gath1, g1_send, g1_recv, f1_send, f1_recv)
    gather_done(gath2, g2_send, g2_recv, f2_send, f2_recv)
    gath2_o[...] = gath2[...]
    gather_done(gath1, g1_send, g1_recv, f1_send, f1_recv)
    gath1_o[...] = gath1[...]


def last_kernel(
    norm,
    field_in,
    field_cot,
    gath1,
    gath2,
    small,
    perm,
    lower,
    upper,
    logs,
    field_in_o,
    field_cot_o,
    kern1_o,
    bias1_o,
    kern2_o,
    bias2_o,
    lower_o,
    upper_o,
    logs_o,
):
    field_in_o[...] = field_in[...]
    field_cot_o[...] = field_cot[...]
    for gath, out, fold in ((gath1, kern1_o, FOLD1), (gath2, kern2_o, FOLD2)):
        hid, ins = out.shape[2], out.shape[3]
        grid = from_blocks(gath[...].astype(F32) * norm, 9 * hid, 9 * ins, fold)
        for k in range(9):
            out[:, k] = grid[:, k * ins : (k + 1) * ins].reshape(9, hid, ins)
    _, _, lower_tri, upper_tri, perm_t, _ = factors(
        perm[...], lower[...], upper[...], logs[...]
    )
    sums = small[...] * norm
    chans = lower.shape[0]
    hid = bias1_o.shape[1]
    mix = jnp.concatenate([sums[:, :chans], sums[:, chans : 2 * chans]], axis=0)
    base = 2 * chans
    bias1_o[...] = sums[0:1, base : base + hid]
    bias2_o[...] = sums[0:1, base + hid : base + 2 * hid]
    turned = dot(perm_t, mix, HIGH)
    lower_full = dot_nt(turned, upper_tri, HIGH)
    upper_full = dot_tn(lower_tri, turned, HIGH)
    rows, cols = iota((chans, chans), 0), iota((chans, chans), 1)
    lower_o[...] = jnp.where(rows > cols, lower_full, 0.0)
    upper_o[...] = jnp.where(cols > rows, upper_full, 0.0)
    diag = jnp.sum(jnp.where(rows == cols, upper_full, 0.0), axis=0, keepdims=True)
    jac_row = sums[0:1, base + 2 * hid : base + 2 * hid + chans]
    logs_o[...] = diag * jnp.exp(logs[...]) + jac_row


def body(
    n,
    out_field,
    out_cot,
    jac_cot,
    mask,
    perm,
    lower_param,
    upper_param,
    log_scale,
    kern1,
    bias1,
    kern2,
    bias2,
):
    chans, count, sites = out_field.shape
    hid = kern1.shape[1]
    chips = n // 2
    perm_row = perm.reshape(1, chans)
    log_row = log_scale.reshape(1, chans)
    _, rows1 = block_rows(9 * hid, 9 * chans, FOLD1, n)
    _, rows2 = block_rows(9 * hid, 9 * hid, FOLD2, n)
    vmem = pl.BlockSpec(memory_space=pltpu.VMEM)
    shape = jax.ShapeDtypeStruct
    field = shape((chans, count, sites), F32)
    dma = pltpu.SemaphoreType.DMA
    field_in, field_cot, gath1, gath2, small = pl.pallas_call(
        functools.partial(main_kernel, n),
        out_shape=(
            field,
            field,
            shape((2, chips, rows1, 128), BF16),
            shape((2, chips, rows2, 128), BF16),
            shape((8, 128), F32),
        ),
        in_specs=[vmem] * 12,
        out_specs=(vmem,) * 5,
        scratch_shapes=[
            pltpu.VMEM((count + 4, chans, sites), BF16),
            pltpu.VMEM((count + 4, 9 * chans, sites), BF16),
            pltpu.VMEM((count + 2, 9 * hid, sites), BF16),
            pltpu.VMEM((count + 2, hid, sites), BF16),
            pltpu.VMEM((count + 2, hid, sites), BF16),
            pltpu.VMEM((9 * hid, 9 * chans), BF16),
            pltpu.VMEM((9 * chans, 9 * hid), BF16),
            pltpu.VMEM((9 * hid, 9 * hid), BF16),
            pltpu.VMEM((9 * hid, 9 * hid), BF16),
        ]
        + [pltpu.VMEM((2, chips, rows1, 128), BF16)] * 2
        + [pltpu.VMEM((chips, rows1, 128), BF16)] * 2
        + [pltpu.VMEM((2, chips, rows2, 128), BF16)] * 2
        + [pltpu.VMEM((chips, rows2, 128), BF16)] * 2
        + [pltpu.VMEM((8, 128), F32)] * 2
        + [pltpu.VMEM((chips, 8, 128), F32)]
        + [dma((2,))] * 3
        + [dma((6,))] * 2
        + [dma((chips,))] * 14,
        compiler_params=pltpu.CompilerParams(
            collective_id=0, has_side_effects=True, vmem_limit_bytes=VMEM_LIMIT
        ),
        name="block_backward",
    )(
        out_field,
        out_cot,
        jac_cot,
        mask,
        perm_row,
        lower_param,
        upper_param,
        log_row,
        kern1.reshape(9, 9, hid, chans),
        bias1.reshape(1, hid),
        kern2.reshape(9, 9, kern2.shape[1], hid),
        bias2.reshape(1, -1),
    )
    norm = 1.0 / math.sqrt(count * sites * n)
    outs = pl.pallas_call(
        functools.partial(last_kernel, norm),
        out_shape=(
            field,
            field,
            shape((9, 9, hid, chans), F32),
            shape((1, hid), F32),
            shape((9, 9, 2 * chans, hid), F32),
            shape((1, 2 * chans), F32),
            shape((chans, chans), F32),
            shape((chans, chans), F32),
            shape((1, chans), F32),
        ),
        in_specs=[vmem] * 9,
        out_specs=(vmem,) * 9,
        compiler_params=pltpu.CompilerParams(vmem_limit_bytes=VMEM_LIMIT),
        name="unpack",
    )(
        field_in,
        field_cot,
        gath1.reshape(n * rows1, 128),
        gath2.reshape(n * rows2, 128),
        small,
        perm_row,
        lower_param,
        upper_param,
        log_row,
    )
    return (
        outs[0],
        outs[1],
        outs[2].reshape(81, hid, chans),
        outs[3].reshape(-1),
        outs[4].reshape(81, 2 * chans, hid),
        outs[5].reshape(-1),
        outs[6],
        outs[7],
        outs[8].reshape(-1),
    )


def solution(mesh):
    split = ("groups", "ta")
    in_specs = (
        P(None, split, None),
        P(None, split, None),
        P(split, None),
        P(split, None),
    ) + (P(),) * 8
    out_specs = (
        P(None, split, None),
        P(None, split, None),
        P("groups", None, None),
        P("groups"),
        P("groups", None, None),
        P("groups"),
        P("groups", None),
        P("groups", None),
        P("groups"),
    )
    return jax.shard_map(
        functools.partial(body, mesh.shape["ta"]),
        mesh=mesh,
        in_specs=in_specs,
        out_specs=out_specs,
        check_vma=False,
    )
```

```python
import functools
import math

import jax
import jax.numpy as jnp
from jax import lax
from jax.experimental import pallas as pl
from jax.experimental.pallas import tpu as pltpu
from jax.sharding import PartitionSpec as P

LX = 8
LY = 8
LZ = 16
ROW = LY * LZ

HIGH = lax.Precision.HIGHEST
F32 = jnp.float32
BF16 = jnp.bfloat16
VMEM_LIMIT = 48 * 1024 * 1024


def dot(a, b, precision=None):
    return lax.dot_general(
        a, b, (((1,), (0,)), ((), ())), precision=precision, preferred_element_type=F32
    )


def dot_tn(a, b, precision=None):
    return lax.dot_general(
        a, b, (((0,), (0,)), ((), ())), precision=precision, preferred_element_type=F32
    )


def dot_nt(a, b, precision=None):
    return lax.dot_general(
        a, b, (((1,), (1,)), ((), ())), precision=precision, preferred_element_type=F32
    )


def split3(v):
    first = v.astype(BF16)
    rest = v - first.astype(F32)
    second = rest.astype(BF16)
    return first, second, (rest - second.astype(F32)).astype(BF16)


def mix_field(matrix, pieces):
    m1, m2, m3 = (m.astype(F32) for m in split3(matrix))
    x1, x2, x3 = pieces
    left = jnp.concatenate([m1, m1, m1, m2, m2, m3], axis=1).astype(BF16)
    return dot(left, jnp.concatenate([x1, x2, x3, x1, x2, x1], axis=0))


def iota(shape, dim):
    return lax.broadcasted_iota(jnp.int32, shape, dim)


def column(row):
    count = row.shape[1]
    same = iota((count, count), 0) == iota((count, count), 1)
    return jnp.sum(jnp.where(same, row, 0.0), axis=1, keepdims=True)


def substitute(strict, values, order):
    for j in order:
        values = values - strict[:, j : j + 1] * values[j : j + 1, :]
    return values


def factors(perm_row, lower_param, upper_param, log_row):
    chans = lower_param.shape[0]
    rows, cols = iota((chans, chans), 0), iota((chans, chans), 1)
    strict_low = jnp.where(rows > cols, lower_param, 0.0)
    strict_up = jnp.where(cols > rows, upper_param, 0.0)
    diag = column(jnp.exp(log_row))
    perm_t = jnp.where(rows == perm_row, 1.0, 0.0)
    lower_tri = strict_low + jnp.where(rows == cols, 1.0, 0.0)
    upper_tri = strict_up + jnp.where(rows == cols, diag, 0.0)
    return strict_low, strict_up, lower_tri, upper_tri, perm_t, diag


def to_tiles(v):
    return jnp.concatenate([v[:, x * ROW : (x + 1) * ROW] for x in range(LX)], axis=0)


def to_lanes(v):
    chans = v.shape[0] // LX
    return jnp.concatenate([v[x * chans : (x + 1) * chans] for x in range(LX)], axis=1)


def shift_z(v, off):
    if off == 0:
        return v
    z = iota(v.shape, 1) % LZ
    if off > 0:
        return jnp.where(z == LZ - 1, pltpu.roll(v, LZ - 1, 1), pltpu.roll(v, ROW - 1, 1))
    return jnp.where(z == 0, pltpu.roll(v, ROW - LZ + 1, 1), pltpu.roll(v, 1, 1))


def shift_y(v, off):
    if off == 0:
        return v
    return pltpu.roll(v, (ROW - off * LZ) % ROW, 1)


def shift_x(v, off):
    if off == 0:
        return v
    if off > 0:
        return jnp.concatenate([v[:, ROW:], v[:, :ROW]], axis=1)
    return jnp.concatenate([v[:, -ROW:], v[:, :-ROW]], axis=1)


def store_plane_stack(ref, slot, v):
    chans = v.shape[0]
    tiles = to_tiles(v)
    along_z = [shift_z(tiles, e) for e in (-1, 0, 1)]
    for c in (-1, 0, 1):
        for e in (-1, 0, 1):
            k = 3 * (c + 1) + e + 1
            piece = to_lanes(shift_y(along_z[e + 1], c)).astype(BF16)
            ref[slot, k * chans : (k + 1) * chans, :] = piece


def unstack_plane(q):
    chans = q.shape[0] // 9
    total = None
    for e in (-1, 0, 1):
        along = None
        for c in (-1, 0, 1):
            k = 3 * (c + 1) + e + 1
            piece = shift_y(to_tiles(q[k * chans : (k + 1) * chans]), -c)
            along = piece if along is None else along + piece
        along = shift_z(along, -e)
        total = along if total is None else total + along
    return to_lanes(total)


def valid_taps(source, count):
    taps = [a for a in (-1, 0, 1) if 0 <= source - a < count]
    return taps[0], taps[-1] + 1


def add_forward(outs, weight, stack, source):
    first, end = valid_taps(source, len(outs))
    hid = weight.shape[0] // 9
    prod = dot(weight[3 * hid * (first + 1) : 3 * hid * (end + 1), :], stack)
    for a in range(first, end):
        for b in (-1, 0, 1):
            lo = (3 * (a - first) + b + 1) * hid
            piece = shift_x(prod[lo : lo + hid], b)
            t = source - a
            outs[t] = piece if outs[t] is None else outs[t] + piece


def spread_stack(slices, taps):
    return jnp.concatenate(
        [shift_x(slices[i], -b) for i in range(len(taps)) for b in (-1, 0, 1)], axis=0
    )


def kernel_grads(cot, stacks, count):
    blocks = {}
    for source in range(-1, count + 1):
        first, end = valid_taps(source, count)
        taps = list(range(first, end))
        left = spread_stack([cot[source - a] for a in taps], taps)
        prod = dot_nt(left, stacks(source))
        for i, a in enumerate(taps):
            size = left.shape[0] // len(taps)
            part = prod[i * size : (i + 1) * size]
            blocks[a] = part if a not in blocks else blocks[a] + part
    return jnp.concatenate([blocks[a] for a in (-1, 0, 1)], axis=0)


def to_blocks(grad, fold):
    rows, cols = grad.shape
    full = cols // 128
    rest = cols - full * 128
    parts = [grad[:, i * 128 : (i + 1) * 128] for i in range(full)]
    tail = grad[:, full * 128 :]
    each = rows // fold
    tails = [tail[i * each : (i + 1) * each] for i in range(fold)]
    tails.append(jnp.zeros((each, 128 - rest * fold), F32))
    parts.append(jnp.concatenate(tails, axis=1))
    return jnp.concatenate(parts, axis=0)


def from_blocks(packed, rows, cols, fold):
    full = cols // 128
    rest = cols - full * 128
    each = rows // fold
    parts = [packed[i * rows : (i + 1) * rows] for i in range(full)]
    last = packed[full * rows : full * rows + each]
    tail = jnp.concatenate([last[:, i * rest : (i + 1) * rest] for i in range(fold)], axis=0)
    return jnp.concatenate(parts + [tail], axis=1)


def block_rows(rows, cols, fold, n):
    total = (cols // 128) * rows + rows // fold
    blocks = -(-total // 16)
    return total, 16 * -(-blocks // n)


FOLD1 = 3
FOLD2 = 1


def main_kernel(
    n,
    out_field,
    out_cot,
    jac,
    mask,
    perm,
    lower,
    upper,
    logs,
    kern1,
    bias1,
    kern2,
    bias2,
    field_in_o,
    field_cot_o,
    gath1_o,
    gath2_o,
    small_o,
    frozen,
    stack1,
    stack2,
    ncot,
    pcot,
    w1,
    w1t,
    w2,
    w2t,
    taps1,
    taps2,
    send1,
    gath1,
    paired1,
    recv1,
    send2,
    gath2,
    paired2,
    recv2,
    small_mine,
    small_other,
    small_all,
    p1_sem,
    p2_sem,
    ps_sem,
    halo_send,
    halo_recv,
    s1_send,
    s1_recv,
    s2_send,
    s2_recv,
    g1_send,
    g1_recv,
    g2_send,
    g2_recv,
    sm_send,
    sm_recv,
    f1_send,
    f1_recv,
    f2_send,
    f2_recv,
):
    me = lax.axis_index("ta")
    chans, count, sites = out_field.shape
    hid = kern1.shape[0]
    right, left = lax.rem(me + 1, n), lax.rem(me + n - 1, n)
    chips = n // 2
    chip, core = me // 2, lax.rem(me, 2)
    other = 1 - core
    partner = 2 * chip + other

    barrier = pltpu.get_barrier_semaphore()

    def greet(k, carry):
        pl.semaphore_signal(barrier, inc=1, device_id={"ta": lax.rem(me + k, n)})
        return carry

    lax.fori_loop(1, n, greet, 0)

    strict_low, strict_up, lower_tri, upper_tri, perm_t, diag = factors(
        perm[...], lower[...], upper[...], logs[...]
    )
    solved = substitute(strict_low, perm_t, range(chans))
    unmixer = substitute(strict_up / diag, solved / diag, range(chans - 1, -1, -1))
    mixer_t = dot_tn(dot(lower_tri, upper_tri, HIGH), perm_t, HIGH)

    keep = [mask[t : t + 1, :].astype(F32) for t in range(count)]
    coupled = [mix_field(unmixer, split3(out_field[:, t, :])) for t in range(count)]
    for t in range(count):
        frozen[2 + t] = (keep[t] * coupled[t]).astype(BF16)

    pl.semaphore_wait(barrier, n - 1)

    def halo(index, src, dst, where):
        return pltpu.make_async_remote_copy(
            src_ref=src,
            dst_ref=dst,
            send_sem=halo_send.at[index],
            recv_sem=halo_recv.at[index],
            device_id={"ta": where},
        )

    def exchange(base, buf, width):
        up = halo(base, buf.at[pl.ds(count, width)], buf.at[pl.ds(0, width)], right)
        down = halo(
            base + 1, buf.at[pl.ds(width, width)], buf.at[pl.ds(width + count, width)], left
        )
        up.start()
        down.start()
        return up, down

    first_halo = exchange(0, frozen, 2)

    def remote(src, dst, send_sem, recv_sem, where):
        return pltpu.make_async_remote_copy(
            src_ref=src,
            dst_ref=dst,
            send_sem=send_sem,
            recv_sem=recv_sem,
            device_id={"ta": where},
        )

    def ahead(k):
        return lax.rem(chip + k, chips)

    def behind(k):
        return lax.rem(chip + chips - k, chips)

    def each(step):
        def run(k, carry):
            step(k)
            return carry

        lax.fori_loop(1, chips, run, 0)

    def pair_copy(send, paired, sems):
        return remote(send.at[other], paired, sems.at[0], sems.at[1], partner)

    def load_send(send, packed):
        rows = send.shape[2]
        for p in range(n):
            send[p // chips, p % chips] = packed[p * rows : (p + 1) * rows]

    def pair_sum(send, paired):
        paired[...] = (send[core].astype(F32) + paired[...].astype(F32)).astype(BF16)

    def scatter_copy(paired, recv, s_sem, r_sem, k):
        return remote(
            paired.at[ahead(k)], recv.at[k], s_sem.at[k], r_sem.at[k], 2 * ahead(k) + core
        )

    def scatter(*refs):
        each(lambda k: scatter_copy(*refs, k).start())

    def collect(paired, recv, s_sem, r_sem):
        def step(k, total):
            scatter_copy(paired, recv, s_sem, r_sem, k).wait()
            return total + recv[k].astype(F32)

        return lax.fori_loop(1, chips, step, paired[chip].astype(F32)).astype(BF16)

    def gather_copy(buf, s_sem, r_sem, k, at):
        return remote(
            buf.at[core, chip], buf.at[core, at], s_sem.at[k], r_sem.at[k], 2 * ahead(k) + core
        )

    def forward_copy(buf, f_send, f_recv, k, to):
        return remote(
            buf.at[core, behind(k)], buf.at[to, behind(k)], f_send.at[k], f_recv.at[k], partner
        )

    def gather(buf, s_sem, r_sem, f_send, f_recv):
        forward_copy(buf, f_send, f_recv, 0, core).start()
        each(lambda k: gather_copy(buf, s_sem, r_sem, k, chip).start())

    def gather_forward(buf, s_sem, r_sem, f_send, f_recv):
        def step(k):
            gather_copy(buf, s_sem, r_sem, k, behind(k)).wait_recv()
            forward_copy(buf, f_send, f_recv, k, core).start()

        each(step)

    def gather_done(buf, s_sem, r_sem, f_send, f_recv):
        def step(k):
            gather_copy(buf, s_sem, r_sem, k, chip).wait_send()
            forward_copy(buf, f_send, f_recv, k, core).wait_send()
            forward_copy(buf, f_send, f_recv, k, other).wait_recv()

        forward_copy(buf, f_send, f_recv, 0, core).wait_send()
        forward_copy(buf, f_send, f_recv, 0, other).wait_recv()
        each(step)

    for kern, taps, w, wt in ((kern1, taps1, w1, w1t), (kern2, taps2, w2, w2t)):
        ins = kern.shape[1]
        flat = kern[...].astype(F32).reshape(hid * ins, 81).T
        for o in range(hid):
            taps[pl.ds(o, 81, stride=hid), :] = flat[:, o * ins : (o + 1) * ins]
        split = taps[...].reshape(9, 9, hid, ins)
        wide = jnp.concatenate(
            [split[:, k].reshape(9 * hid, ins) for k in range(9)], axis=1
        )
        w[...] = wide.astype(BF16)
        wt[...] = wide.T.astype(BF16)

    cot_pieces = [split3(out_cot[:, t, :]) for t in range(count)]
    coupled_cot = [mix_field(mixer_t, cot_pieces[t]) for t in range(count)]
    wide_mix = None
    for t in range(count):
        term = dot_nt(
            jnp.concatenate(cot_pieces[t], axis=0),
            jnp.concatenate(split3(coupled[t]), axis=0),
        )
        wide_mix = term if wide_mix is None else wide_mix + term
    mix = None
    for i, j in ((2, 0), (1, 1), (0, 2), (1, 0), (0, 1), (0, 0)):
        term = wide_mix[i * chans : (i + 1) * chans, j * chans : (j + 1) * chans]
        mix = term if mix is None else mix + term
    jac_sum = jnp.sum(jnp.sum(jac[...], axis=1, keepdims=True), axis=0, keepdims=True)

    hidden_pre = [None] * (count + 2)
    for slot in range(2, count + 2):
        store_plane_stack(stack1, slot, frozen[slot].astype(F32))
        add_forward(hidden_pre, w1, stack1[slot], slot - 1)
    for copy in first_halo:
        copy.wait()
    for slot in [0, 1] + [count + 2, count + 3]:
        store_plane_stack(stack1, slot, frozen[slot].astype(F32))
        add_forward(hidden_pre, w1, stack1[slot], slot - 1)

    bias1_col = column(bias1[...])
    bias2_col = column(bias2[...])
    net = [None] * count
    hidden_mid = []
    for slot in range(count + 2):
        hidden = jnp.tanh(hidden_pre[slot] + bias1_col).astype(BF16).astype(F32)
        if 1 <= slot <= count:
            hidden_mid.append(hidden)
        store_plane_stack(stack2, slot, hidden)
        add_forward(net, w2, stack2[slot], slot - 1)

    growth = []
    cots = []
    for t in range(count):
        net_t = net[t] + bias2_col
        scale = jnp.tanh(net_t[:chans])
        shift = net_t[chans:]
        free = 1.0 - keep[t]
        grow = jnp.exp(scale)
        growth.append(grow)
        fin = keep[t] * coupled[t] + free * (coupled[t] - shift) * jnp.exp(-scale)
        field_in_o[:, t, :] = fin
        scale_cot = free * (coupled_cot[t] * fin * grow + jac[t : t + 1, :])
        cot = jnp.concatenate(
            [scale_cot * (1.0 - scale * scale), free * coupled_cot[t]], axis=0
        ).astype(BF16)
        ncot[1 + t] = cot
        cots.append(cot)
    second_halo = exchange(2, ncot, 1)

    grads2 = kernel_grads(cots, lambda s: stack2[s + 1], count)
    total2, rows2 = block_rows(9 * hid, 9 * hid, FOLD2, n)
    packed2 = to_blocks(grads2, FOLD2)
    packed2 = jnp.concatenate(
        [packed2, jnp.zeros((n * rows2 - total2, 128), F32)], axis=0
    ).astype(BF16)
    load_send(send2, packed2)
    pair2 = pair_copy(send2, paired2, p2_sem)
    pair2.start()

    ones = jnp.ones((8, sites), BF16)
    bias2_row = sum(dot_nt(ones, c) for c in cots)

    for copy in second_halo:
        copy.wait()
    pres = []
    for t in range(count):
        taps = (-1, 0, 1)
        wide = spread_stack([ncot[1 + t - a] for a in taps], taps)
        hidden_cot = unstack_plane(dot(w2t[...], wide))
        pre = (hidden_cot * (1.0 - hidden_mid[t] * hidden_mid[t])).astype(BF16)
        pcot[1 + t] = pre
        pres.append(pre)
    third_halo = exchange(4, pcot, 1)

    pair2.wait()
    pair_sum(send2, paired2)
    scatter(paired2, recv2, s2_send, s2_recv)

    grads1 = kernel_grads(pres, lambda s: stack1[s + 2], count)
    total1, rows1 = block_rows(9 * hid, 9 * chans, FOLD1, n)
    packed1 = to_blocks(grads1, FOLD1)
    packed1 = jnp.concatenate(
        [packed1, jnp.zeros((n * rows1 - total1, 128), F32)], axis=0
    ).astype(BF16)
    load_send(send1, packed1)
    pair1 = pair_copy(send1, paired1, p1_sem)
    pair1.start()

    bias1_row = sum(dot_nt(ones, c) for c in pres)
    small_mine[...] = jnp.concatenate(
        [mix[:8], mix[8:], bias1_row, bias2_row, jnp.broadcast_to(jac_sum, (8, 32))], axis=1
    )
    pair_small = remote(small_mine, small_other, ps_sem.at[0], ps_sem.at[1], partner)
    pair_small.start()

    pair1.wait()
    pair_sum(send1, paired1)
    scatter(paired1, recv1, s1_send, s1_recv)
    pair_small.wait()
    small_all[chip] = small_mine[...] + small_other[...]

    def small_copy(k, at):
        return remote(
            small_all.at[chip],
            small_all.at[at],
            sm_send.at[k],
            sm_recv.at[k],
            2 * ahead(k) + core,
        )

    each(lambda k: small_copy(k, chip).start())

    gath2[core, chip] = collect(paired2, recv2, s2_send, s2_recv)
    gather(gath2, g2_send, g2_recv, f2_send, f2_recv)

    for copy in third_halo:
        copy.wait()
    for t in range(count):
        taps = (-1, 0, 1)
        wide = spread_stack([pcot[1 + t - a] for a in taps], taps)
        frozen_cot = unstack_plane(dot(w1t[...], wide))
        free = 1.0 - keep[t]
        field_cot_o[:, t, :] = (
            keep[t] * (coupled_cot[t] + frozen_cot) + free * coupled_cot[t] * growth[t]
        )

    gath1[core, chip] = collect(paired1, recv1, s1_send, s1_recv)
    gather(gath1, g1_send, g1_recv, f1_send, f1_recv)

    gather_forward(gath2, g2_send, g2_recv, f2_send, f2_recv)

    def small_done(k):
        small_copy(k, chip).wait_send()
        small_copy(k, behind(k)).wait_recv()

    each(small_done)
    small_o[...] = lax.fori_loop(
        0, chips, lambda k, total: total + small_all[k], jnp.zeros(small_mine.shape, F32)
    )

    gather_forward(gath1, g1_send, g1_recv, f1_send, f1_recv)
    gather_done(gath2, g2_send, g2_recv, f2_send, f2_recv)
    gath2_o[...] = gath2[...]
    gather_done(gath1, g1_send, g1_recv, f1_send, f1_recv)
    gath1_o[...] = gath1[...]


def last_kernel(
    norm,
    field_in,
    field_cot,
    gath1,
    gath2,
    small,
    perm,
    lower,
    upper,
    logs,
    field_in_o,
    field_cot_o,
    kern1_o,
    bias1_o,
    kern2_o,
    bias2_o,
    lower_o,
    upper_o,
    logs_o,
    taps1,
    taps2,
):
    field_in_o[...] = field_in[...]
    field_cot_o[...] = field_cot[...]
    for gath, out, taps, fold in (
        (gath1, kern1_o, taps1, FOLD1),
        (gath2, kern2_o, taps2, FOLD2),
    ):
        hid, ins = out.shape[0], out.shape[1]
        grid = from_blocks(gath[...].astype(F32) * norm, 9 * hid, 9 * ins, fold)
        for k in range(9):
            for x in range(9):
                start = (9 * x + k) * hid
                taps[start : start + hid, :] = grid[
                    x * hid : (x + 1) * hid, k * ins : (k + 1) * ins
                ]
        flat = jnp.concatenate([taps[pl.ds(o, 81, stride=hid), :] for o in range(hid)], axis=1)
        out[...] = flat.T.reshape(hid, ins, 81)
    _, _, lower_tri, upper_tri, perm_t, _ = factors(
        perm[...], lower[...], upper[...], logs[...]
    )
    sums = small[...] * norm
    chans = lower.shape[0]
    hid = bias1_o.shape[1]
    mix = jnp.concatenate([sums[:, :chans], sums[:, chans : 2 * chans]], axis=0)
    base = 2 * chans
    bias1_o[...] = sums[0:1, base : base + hid]
    bias2_o[...] = sums[0:1, base + hid : base + 2 * hid]
    turned = dot(perm_t, mix, HIGH)
    lower_full = dot_nt(turned, upper_tri, HIGH)
    upper_full = dot_tn(lower_tri, turned, HIGH)
    rows, cols = iota((chans, chans), 0), iota((chans, chans), 1)
    lower_o[...] = jnp.where(rows > cols, lower_full, 0.0)
    upper_o[...] = jnp.where(cols > rows, upper_full, 0.0)
    diag = jnp.sum(jnp.where(rows == cols, upper_full, 0.0), axis=0, keepdims=True)
    jac_row = sums[0:1, base + 2 * hid : base + 2 * hid + chans]
    logs_o[...] = diag * jnp.exp(logs[...]) + jac_row


def body(
    n,
    out_field,
    out_cot,
    jac_cot,
    mask,
    perm,
    lower_param,
    upper_param,
    log_scale,
    kern1,
    bias1,
    kern2,
    bias2,
):
    chans, count, sites = out_field.shape
    hid = kern1.shape[1]
    chips = n // 2
    perm_row = perm.reshape(1, chans)
    log_row = log_scale.reshape(1, chans)
    _, rows1 = block_rows(9 * hid, 9 * chans, FOLD1, n)
    _, rows2 = block_rows(9 * hid, 9 * hid, FOLD2, n)
    vmem = pl.BlockSpec(memory_space=pltpu.VMEM)
    shape = jax.ShapeDtypeStruct
    field = shape((chans, count, sites), F32)
    dma = pltpu.SemaphoreType.DMA
    field_in, field_cot, gath1, gath2, small = pl.pallas_call(
        functools.partial(main_kernel, n),
        out_shape=(
            field,
            field,
            shape((2, chips, rows1, 128), BF16),
            shape((2, chips, rows2, 128), BF16),
            shape((8, 128), F32),
        ),
        in_specs=[vmem] * 12,
        out_specs=(vmem,) * 5,
        scratch_shapes=[
            pltpu.VMEM((count + 4, chans, sites), BF16),
            pltpu.VMEM((count + 4, 9 * chans, sites), BF16),
            pltpu.VMEM((count + 2, 9 * hid, sites), BF16),
            pltpu.VMEM((count + 2, hid, sites), BF16),
            pltpu.VMEM((count + 2, hid, sites), BF16),
            pltpu.VMEM((9 * hid, 9 * chans), BF16),
            pltpu.VMEM((9 * chans, 9 * hid), BF16),
            pltpu.VMEM((9 * hid, 9 * hid), BF16),
            pltpu.VMEM((9 * hid, 9 * hid), BF16),
            pltpu.VMEM((81 * hid, chans), F32),
            pltpu.VMEM((81 * hid, hid), F32),
        ]
        + [pltpu.VMEM((2, chips, rows1, 128), BF16)] * 2
        + [pltpu.VMEM((chips, rows1, 128), BF16)] * 2
        + [pltpu.VMEM((2, chips, rows2, 128), BF16)] * 2
        + [pltpu.VMEM((chips, rows2, 128), BF16)] * 2
        + [pltpu.VMEM((8, 128), F32)] * 2
        + [pltpu.VMEM((chips, 8, 128), F32)]
        + [dma((2,))] * 3
        + [dma((6,))] * 2
        + [dma((chips,))] * 14,
        compiler_params=pltpu.CompilerParams(
            collective_id=0, has_side_effects=True, vmem_limit_bytes=VMEM_LIMIT
        ),
        name="block_backward",
    )(
        out_field,
        out_cot,
        jac_cot,
        mask,
        perm_row,
        lower_param,
        upper_param,
        log_row,
        kern1.transpose(1, 2, 0),
        bias1.reshape(1, hid),
        kern2.transpose(1, 2, 0),
        bias2.reshape(1, -1),
    )
    norm = 1.0 / math.sqrt(count * sites * n)
    outs = pl.pallas_call(
        functools.partial(last_kernel, norm),
        out_shape=(
            field,
            field,
            shape((hid, chans, 81), F32),
            shape((1, hid), F32),
            shape((2 * chans, hid, 81), F32),
            shape((1, 2 * chans), F32),
            shape((chans, chans), F32),
            shape((chans, chans), F32),
            shape((1, chans), F32),
        ),
        in_specs=[vmem] * 9,
        out_specs=(vmem,) * 9,
        scratch_shapes=[
            pltpu.VMEM((81 * hid, chans), F32),
            pltpu.VMEM((162 * chans, hid), F32),
        ],
        compiler_params=pltpu.CompilerParams(vmem_limit_bytes=VMEM_LIMIT),
        name="unpack",
    )(
        field_in,
        field_cot,
        gath1.reshape(n * rows1, 128),
        gath2.reshape(n * rows2, 128),
        small,
        perm_row,
        lower_param,
        upper_param,
        log_row,
    )
    return (
        outs[0],
        outs[1],
        outs[2].transpose(2, 0, 1),
        outs[3].reshape(-1),
        outs[4].transpose(2, 0, 1),
        outs[5].reshape(-1),
        outs[6],
        outs[7],
        outs[8].reshape(-1),
    )


def solution(mesh):
    split = ("groups", "ta")
    in_specs = (
        P(None, split, None),
        P(None, split, None),
        P(split, None),
        P(split, None),
    ) + (P(),) * 8
    out_specs = (
        P(None, split, None),
        P(None, split, None),
        P("groups", None, None),
        P("groups"),
        P("groups", None, None),
        P("groups"),
        P("groups", None),
        P("groups", None),
        P("groups"),
    )
    return jax.shard_map(
        functools.partial(body, mesh.shape["ta"]),
        mesh=mesh,
        in_specs=in_specs,
        out_specs=out_specs,
        check_vma=False,
    )
```

```python
import functools
import math

import jax
import jax.numpy as jnp
from jax import lax
from jax.experimental import pallas as pl
from jax.experimental.pallas import tpu as pltpu
from jax.sharding import PartitionSpec as P

LX = 8
LY = 8
LZ = 16
ROW = LY * LZ

HIGH = lax.Precision.HIGHEST
F32 = jnp.float32
BF16 = jnp.bfloat16
VMEM_LIMIT = 63 * 1024 * 1024


def dot(a, b, precision=None):
    return lax.dot_general(
        a, b, (((1,), (0,)), ((), ())), precision=precision, preferred_element_type=F32
    )


def dot_tn(a, b, precision=None):
    return lax.dot_general(
        a, b, (((0,), (0,)), ((), ())), precision=precision, preferred_element_type=F32
    )


def dot_nt(a, b, precision=None):
    return lax.dot_general(
        a, b, (((1,), (1,)), ((), ())), precision=precision, preferred_element_type=F32
    )


def split3(v):
    first = v.astype(BF16)
    rest = v - first.astype(F32)
    second = rest.astype(BF16)
    return first, second, (rest - second.astype(F32)).astype(BF16)


def mix_field(matrix, pieces):
    m1, m2, m3 = (m.astype(F32) for m in split3(matrix))
    x1, x2, x3 = pieces
    left = jnp.concatenate([m1, m1, m1, m2, m2, m3], axis=1).astype(BF16)
    return dot(left, jnp.concatenate([x1, x2, x3, x1, x2, x1], axis=0))


def iota(shape, dim):
    return lax.broadcasted_iota(jnp.int32, shape, dim)


def column(row):
    count = row.shape[1]
    same = iota((count, count), 0) == iota((count, count), 1)
    return jnp.sum(jnp.where(same, row, 0.0), axis=1, keepdims=True)


def substitute(strict, values, order):
    for j in order:
        values = values - strict[:, j : j + 1] * values[j : j + 1, :]
    return values


def factors(perm_row, lower_param, upper_param, log_row):
    chans = lower_param.shape[0]
    rows, cols = iota((chans, chans), 0), iota((chans, chans), 1)
    strict_low = jnp.where(rows > cols, lower_param, 0.0)
    strict_up = jnp.where(cols > rows, upper_param, 0.0)
    diag = column(jnp.exp(log_row))
    perm_t = jnp.where(rows == perm_row, 1.0, 0.0)
    lower_tri = strict_low + jnp.where(rows == cols, 1.0, 0.0)
    upper_tri = strict_up + jnp.where(rows == cols, diag, 0.0)
    return strict_low, strict_up, lower_tri, upper_tri, perm_t, diag


def to_tiles(v):
    return jnp.concatenate([v[:, x * ROW : (x + 1) * ROW] for x in range(LX)], axis=0)


def to_lanes(v):
    chans = v.shape[0] // LX
    return jnp.concatenate([v[x * chans : (x + 1) * chans] for x in range(LX)], axis=1)


def shift_z(v, off):
    if off == 0:
        return v
    z = iota(v.shape, 1) % LZ
    if off > 0:
        return jnp.where(z == LZ - 1, pltpu.roll(v, LZ - 1, 1), pltpu.roll(v, ROW - 1, 1))
    return jnp.where(z == 0, pltpu.roll(v, ROW - LZ + 1, 1), pltpu.roll(v, 1, 1))


def shift_y(v, off):
    if off == 0:
        return v
    return pltpu.roll(v, (ROW - off * LZ) % ROW, 1)


def shift_x(v, off):
    if off == 0:
        return v
    if off > 0:
        return jnp.concatenate([v[:, ROW:], v[:, :ROW]], axis=1)
    return jnp.concatenate([v[:, -ROW:], v[:, :-ROW]], axis=1)


def store_plane_stack(ref, slot, v):
    chans = v.shape[0]
    tiles = to_tiles(v)
    along_z = [shift_z(tiles, e) for e in (-1, 0, 1)]
    for c in (-1, 0, 1):
        for e in (-1, 0, 1):
            k = 3 * (c + 1) + e + 1
            piece = to_lanes(shift_y(along_z[e + 1], c)).astype(BF16)
            ref[slot, k * chans : (k + 1) * chans, :] = piece


def unstack_plane(q):
    chans = q.shape[0] // 9
    total = None
    for e in (-1, 0, 1):
        along = None
        for c in (-1, 0, 1):
            k = 3 * (c + 1) + e + 1
            piece = shift_y(to_tiles(q[k * chans : (k + 1) * chans]), -c)
            along = piece if along is None else along + piece
        along = shift_z(along, -e)
        total = along if total is None else total + along
    return to_lanes(total)


def valid_taps(source, count):
    taps = [a for a in (-1, 0, 1) if 0 <= source - a < count]
    return taps[0], taps[-1] + 1


def add_forward(outs, weight, stack, source):
    first, end = valid_taps(source, len(outs))
    hid = weight.shape[0] // 9
    prod = dot(weight[3 * hid * (first + 1) : 3 * hid * (end + 1), :], stack)
    for a in range(first, end):
        for b in (-1, 0, 1):
            lo = (3 * (a - first) + b + 1) * hid
            piece = shift_x(prod[lo : lo + hid], b)
            t = source - a
            outs[t] = piece if outs[t] is None else outs[t] + piece


def spread_stack(slices, taps):
    return jnp.concatenate(
        [shift_x(slices[i], -b) for i in range(len(taps)) for b in (-1, 0, 1)], axis=0
    )


def kernel_grads(cot, stacks, count):
    blocks = {}
    for source in range(-1, count + 1):
        first, end = valid_taps(source, count)
        taps = list(range(first, end))
        left = spread_stack([cot[source - a] for a in taps], taps)
        prod = dot_nt(left, stacks(source))
        for i, a in enumerate(taps):
            size = left.shape[0] // len(taps)
            part = prod[i * size : (i + 1) * size]
            blocks[a] = part if a not in blocks else blocks[a] + part
    return jnp.concatenate([blocks[a] for a in (-1, 0, 1)], axis=0)


def to_blocks(grad, fold):
    rows, cols = grad.shape
    full = cols // 128
    rest = cols - full * 128
    parts = [grad[:, i * 128 : (i + 1) * 128] for i in range(full)]
    tail = grad[:, full * 128 :]
    each = rows // fold
    tails = [tail[i * each : (i + 1) * each] for i in range(fold)]
    tails.append(jnp.zeros((each, 128 - rest * fold), F32))
    parts.append(jnp.concatenate(tails, axis=1))
    return jnp.concatenate(parts, axis=0)


def from_blocks(packed, rows, cols, fold):
    full = cols // 128
    rest = cols - full * 128
    each = rows // fold
    parts = [packed[i * rows : (i + 1) * rows] for i in range(full)]
    last = packed[full * rows : full * rows + each]
    tail = jnp.concatenate([last[:, i * rest : (i + 1) * rest] for i in range(fold)], axis=0)
    return jnp.concatenate(parts + [tail], axis=1)


def block_rows(rows, cols, fold, n):
    total = (cols // 128) * rows + rows // fold
    blocks = -(-total // 16)
    return total, 16 * -(-blocks // n)


FOLD1 = 3
FOLD2 = 1


def unpack_grad(packed, taps, hid, ins, fold, norm):
    grid = from_blocks(packed.astype(F32) * norm, 9 * hid, 9 * ins, fold)
    for k in range(9):
        for x in range(9):
            start = (9 * x + k) * hid
            taps[start : start + hid, :] = grid[
                x * hid : (x + 1) * hid, k * ins : (k + 1) * ins
            ]
    flat = jnp.concatenate([taps[pl.ds(o, 81, stride=hid), :] for o in range(hid)], axis=1)
    return flat.T.reshape(hid, ins, 81)


def main_kernel(n, norm, *refs):
    given, refs = refs[:12], refs[12:]
    held, rest = refs[5:17], refs[:5] + refs[17:-1]
    in_sem = refs[-1]
    loads = [
        pltpu.make_async_copy(src, dst, in_sem.at[i])
        for i, (src, dst) in enumerate(zip(given, held))
    ]
    for i in (5, 6, 7, 4, 0, 3, 8, 10, 1, 2, 9, 11):
        loads[i].start()
    compute(n, norm, loads, *held, *rest)


def compute(
    n,
    norm,
    loads,
    out_field,
    out_cot,
    jac,
    mask,
    perm,
    lower,
    upper,
    logs,
    kern1,
    bias1,
    kern2,
    bias2,
    field_in_o,
    field_cot_o,
    gath1_o,
    kern2_o,
    small_o,
    frozen,
    stack1,
    stack2,
    ncot,
    pcot,
    w1,
    w1t,
    w2,
    w2t,
    taps1,
    taps2,
    send1,
    gath1,
    paired1,
    recv1,
    send2,
    gath2,
    paired2,
    recv2,
    small_mine,
    small_other,
    small_all,
    p1_sem,
    p2_sem,
    ps_sem,
    halo_send,
    halo_recv,
    s1_send,
    s1_recv,
    s2_send,
    s2_recv,
    g1_send,
    g1_recv,
    g2_send,
    g2_recv,
    sm_send,
    sm_recv,
    f1_send,
    f1_recv,
    f2_send,
    f2_recv,
):
    me = lax.axis_index("ta")
    chans, count, sites = out_field.shape
    hid = kern1.shape[0]
    right, left = lax.rem(me + 1, n), lax.rem(me + n - 1, n)
    chips = n // 2
    chip, core = me // 2, lax.rem(me, 2)
    other = 1 - core
    partner = 2 * chip + other

    barrier = pltpu.get_barrier_semaphore()

    def greet(k, carry):
        pl.semaphore_signal(barrier, inc=1, device_id={"ta": lax.rem(me + k, n)})
        return carry

    lax.fori_loop(1, n, greet, 0)

    for i in (4, 5, 6, 7):
        loads[i].wait()
    strict_low, strict_up, lower_tri, upper_tri, perm_t, diag = factors(
        perm[...], lower[...], upper[...], logs[...]
    )
    solved = substitute(strict_low, perm_t, range(chans))
    unmixer = substitute(strict_up / diag, solved / diag, range(chans - 1, -1, -1))
    mixer_t = dot_tn(dot(lower_tri, upper_tri, HIGH), perm_t, HIGH)

    for i in (0, 3):
        loads[i].wait()
    keep = [mask[t : t + 1, :].astype(F32) for t in range(count)]
    coupled = [mix_field(unmixer, split3(out_field[:, t, :])) for t in range(count)]
    for t in range(count):
        frozen[2 + t] = (keep[t] * coupled[t]).astype(BF16)

    pl.semaphore_wait(barrier, n - 1)

    def halo(index, src, dst, where):
        return pltpu.make_async_remote_copy(
            src_ref=src,
            dst_ref=dst,
            send_sem=halo_send.at[index],
            recv_sem=halo_recv.at[index],
            device_id={"ta": where},
        )

    def exchange(base, buf, width):
        up = halo(base, buf.at[pl.ds(count, width)], buf.at[pl.ds(0, width)], right)
        down = halo(
            base + 1, buf.at[pl.ds(width, width)], buf.at[pl.ds(width + count, width)], left
        )
        up.start()
        down.start()
        return up, down

    first_halo = exchange(0, frozen, 2)

    def remote(src, dst, send_sem, recv_sem, where):
        return pltpu.make_async_remote_copy(
            src_ref=src,
            dst_ref=dst,
            send_sem=send_sem,
            recv_sem=recv_sem,
            device_id={"ta": where},
        )

    def ahead(k):
        return lax.rem(chip + k, chips)

    def behind(k):
        return lax.rem(chip + chips - k, chips)

    def each(step):
        def run(k, carry):
            step(k)
            return carry

        lax.fori_loop(1, chips, run, 0)

    def pair_copy(send, paired, sems):
        return remote(send.at[other], paired, sems.at[0], sems.at[1], partner)

    def load_send(send, packed):
        rows = send.shape[2]
        for p in range(n):
            send[p // chips, p % chips] = packed[p * rows : (p + 1) * rows]

    def pair_sum(send, paired):
        paired[...] = (send[core].astype(F32) + paired[...].astype(F32)).astype(BF16)

    def scatter_copy(paired, recv, s_sem, r_sem, k):
        return remote(
            paired.at[ahead(k)], recv.at[k], s_sem.at[k], r_sem.at[k], 2 * ahead(k) + core
        )

    def scatter(*refs):
        each(lambda k: scatter_copy(*refs, k).start())

    def collect(paired, recv, s_sem, r_sem):
        def step(k, total):
            scatter_copy(paired, recv, s_sem, r_sem, k).wait()
            return total + recv[k].astype(F32)

        return lax.fori_loop(1, chips, step, paired[chip].astype(F32)).astype(BF16)

    def gather_copy(buf, s_sem, r_sem, k, at):
        return remote(
            buf.at[core, chip], buf.at[core, at], s_sem.at[k], r_sem.at[k], 2 * ahead(k) + core
        )

    def forward_copy(buf, f_send, f_recv, k, to):
        return remote(
            buf.at[core, behind(k)], buf.at[to, behind(k)], f_send.at[k], f_recv.at[k], partner
        )

    def gather(buf, s_sem, r_sem, f_send, f_recv):
        forward_copy(buf, f_send, f_recv, 0, core).start()
        each(lambda k: gather_copy(buf, s_sem, r_sem, k, chip).start())

    def gather_forward(buf, s_sem, r_sem, f_send, f_recv):
        def step(k):
            gather_copy(buf, s_sem, r_sem, k, behind(k)).wait_recv()
            forward_copy(buf, f_send, f_recv, k, core).start()

        each(step)

    def gather_done(buf, s_sem, r_sem, f_send, f_recv):
        def step(k):
            gather_copy(buf, s_sem, r_sem, k, chip).wait_send()
            forward_copy(buf, f_send, f_recv, k, core).wait_send()
            forward_copy(buf, f_send, f_recv, k, other).wait_recv()

        forward_copy(buf, f_send, f_recv, 0, core).wait_send()
        forward_copy(buf, f_send, f_recv, 0, other).wait_recv()
        each(step)

    for i in (8, 10, 1, 2, 9, 11):
        loads[i].wait()
    for kern, taps, w, wt in ((kern1, taps1, w1, w1t), (kern2, taps2, w2, w2t)):
        ins = kern.shape[1]
        flat = kern[...].astype(F32).reshape(hid * ins, 81).T
        for o in range(hid):
            taps[pl.ds(o, 81, stride=hid), :] = flat[:, o * ins : (o + 1) * ins]
        split = taps[...].reshape(9, 9, hid, ins)
        wide = jnp.concatenate(
            [split[:, k].reshape(9 * hid, ins) for k in range(9)], axis=1
        )
        w[...] = wide.astype(BF16)
        wt[...] = wide.T.astype(BF16)

    cot_pieces = [split3(out_cot[:, t, :]) for t in range(count)]
    coupled_cot = [mix_field(mixer_t, cot_pieces[t]) for t in range(count)]
    wide_mix = None
    for t in range(count):
        term = dot_nt(
            jnp.concatenate(cot_pieces[t], axis=0),
            jnp.concatenate(split3(coupled[t]), axis=0),
        )
        wide_mix = term if wide_mix is None else wide_mix + term
    mix = None
    for i, j in ((2, 0), (1, 1), (0, 2), (1, 0), (0, 1), (0, 0)):
        term = wide_mix[i * chans : (i + 1) * chans, j * chans : (j + 1) * chans]
        mix = term if mix is None else mix + term
    jac_sum = jnp.sum(jnp.sum(jac[...], axis=1, keepdims=True), axis=0, keepdims=True)

    hidden_pre = [None] * (count + 2)
    for slot in range(2, count + 2):
        store_plane_stack(stack1, slot, frozen[slot].astype(F32))
        add_forward(hidden_pre, w1, stack1[slot], slot - 1)
    for copy in first_halo:
        copy.wait()
    for slot in [0, 1] + [count + 2, count + 3]:
        store_plane_stack(stack1, slot, frozen[slot].astype(F32))
        add_forward(hidden_pre, w1, stack1[slot], slot - 1)

    bias1_col = column(bias1[...])
    bias2_col = column(bias2[...])
    net = [None] * count
    hidden_mid = []
    for slot in range(count + 2):
        hidden = jnp.tanh(hidden_pre[slot] + bias1_col).astype(BF16).astype(F32)
        if 1 <= slot <= count:
            hidden_mid.append(hidden)
        store_plane_stack(stack2, slot, hidden)
        add_forward(net, w2, stack2[slot], slot - 1)

    growth = []
    cots = []
    for t in range(count):
        net_t = net[t] + bias2_col
        scale = jnp.tanh(net_t[:chans])
        shift = net_t[chans:]
        free = 1.0 - keep[t]
        grow = jnp.exp(scale)
        growth.append(grow)
        fin = keep[t] * coupled[t] + free * (coupled[t] - shift) * jnp.exp(-scale)
        field_in_o[:, t, :] = fin
        scale_cot = free * (coupled_cot[t] * fin * grow + jac[t : t + 1, :])
        cot = jnp.concatenate(
            [scale_cot * (1.0 - scale * scale), free * coupled_cot[t]], axis=0
        ).astype(BF16)
        ncot[1 + t] = cot
        cots.append(cot)
    second_halo = exchange(2, ncot, 1)

    grads2 = kernel_grads(cots, lambda s: stack2[s + 1], count)
    total2, rows2 = block_rows(9 * hid, 9 * hid, FOLD2, n)
    packed2 = to_blocks(grads2, FOLD2)
    packed2 = jnp.concatenate(
        [packed2, jnp.zeros((n * rows2 - total2, 128), F32)], axis=0
    ).astype(BF16)
    load_send(send2, packed2)
    pair2 = pair_copy(send2, paired2, p2_sem)
    pair2.start()

    ones = jnp.ones((8, sites), BF16)
    bias2_row = sum(dot_nt(ones, c) for c in cots)

    for copy in second_halo:
        copy.wait()
    pres = []
    for t in range(count):
        taps = (-1, 0, 1)
        wide = spread_stack([ncot[1 + t - a] for a in taps], taps)
        hidden_cot = unstack_plane(dot(w2t[...], wide))
        pre = (hidden_cot * (1.0 - hidden_mid[t] * hidden_mid[t])).astype(BF16)
        pcot[1 + t] = pre
        pres.append(pre)
    third_halo = exchange(4, pcot, 1)

    pair2.wait()
    pair_sum(send2, paired2)
    scatter(paired2, recv2, s2_send, s2_recv)

    grads1 = kernel_grads(pres, lambda s: stack1[s + 2], count)
    total1, rows1 = block_rows(9 * hid, 9 * chans, FOLD1, n)
    packed1 = to_blocks(grads1, FOLD1)
    packed1 = jnp.concatenate(
        [packed1, jnp.zeros((n * rows1 - total1, 128), F32)], axis=0
    ).astype(BF16)
    load_send(send1, packed1)
    pair1 = pair_copy(send1, paired1, p1_sem)
    pair1.start()

    bias1_row = sum(dot_nt(ones, c) for c in pres)
    small_mine[...] = jnp.concatenate(
        [mix[:8], mix[8:], bias1_row, bias2_row, jnp.broadcast_to(jac_sum, (8, 32))], axis=1
    )
    pair_small = remote(small_mine, small_other, ps_sem.at[0], ps_sem.at[1], partner)
    pair_small.start()

    pair1.wait()
    pair_sum(send1, paired1)
    scatter(paired1, recv1, s1_send, s1_recv)
    pair_small.wait()
    small_all[chip] = small_mine[...] + small_other[...]

    def small_copy(k, at):
        return remote(
            small_all.at[chip],
            small_all.at[at],
            sm_send.at[k],
            sm_recv.at[k],
            2 * ahead(k) + core,
        )

    each(lambda k: small_copy(k, chip).start())

    gath2[core, chip] = collect(paired2, recv2, s2_send, s2_recv)
    gather(gath2, g2_send, g2_recv, f2_send, f2_recv)

    for copy in third_halo:
        copy.wait()
    for t in range(count):
        taps = (-1, 0, 1)
        wide = spread_stack([pcot[1 + t - a] for a in taps], taps)
        frozen_cot = unstack_plane(dot(w1t[...], wide))
        free = 1.0 - keep[t]
        field_cot_o[:, t, :] = (
            keep[t] * (coupled_cot[t] + frozen_cot) + free * coupled_cot[t] * growth[t]
        )

    gath1[core, chip] = collect(paired1, recv1, s1_send, s1_recv)
    gather(gath1, g1_send, g1_recv, f1_send, f1_recv)

    gather_forward(gath2, g2_send, g2_recv, f2_send, f2_recv)
    gather_done(gath2, g2_send, g2_recv, f2_send, f2_recv)
    kern2_o[...] = unpack_grad(
        gath2[...].reshape(n * rows2, 128), taps2, hid, hid, FOLD2, norm
    )

    def small_done(k):
        small_copy(k, chip).wait_send()
        small_copy(k, behind(k)).wait_recv()

    each(small_done)
    small_o[...] = lax.fori_loop(
        0, chips, lambda k, total: total + small_all[k], jnp.zeros(small_mine.shape, F32)
    )

    gather_forward(gath1, g1_send, g1_recv, f1_send, f1_recv)
    gather_done(gath1, g1_send, g1_recv, f1_send, f1_recv)
    gath1_o[...] = gath1[...]


def last_kernel(
    norm,
    field_in,
    field_cot,
    gath1,
    kern2,
    small,
    perm,
    lower,
    upper,
    logs,
    field_in_o,
    field_cot_o,
    kern1_o,
    bias1_o,
    kern2_o,
    bias2_o,
    lower_o,
    upper_o,
    logs_o,
    taps1,
    out_sem,
):
    moves = [
        pltpu.make_async_copy(src, dst, out_sem.at[i])
        for i, (src, dst) in enumerate(
            ((kern2, kern2_o), (field_in, field_in_o), (field_cot, field_cot_o))
        )
    ]
    for move in moves:
        move.start()
    hid, ins = kern1_o.shape[0], kern1_o.shape[1]
    kern1_o[...] = unpack_grad(gath1[...], taps1, hid, ins, FOLD1, norm)
    _, _, lower_tri, upper_tri, perm_t, _ = factors(
        perm[...], lower[...], upper[...], logs[...]
    )
    sums = small[...] * norm
    chans = lower.shape[0]
    hid = bias1_o.shape[1]
    mix = jnp.concatenate([sums[:, :chans], sums[:, chans : 2 * chans]], axis=0)
    base = 2 * chans
    bias1_o[...] = sums[0:1, base : base + hid]
    bias2_o[...] = sums[0:1, base + hid : base + 2 * hid]
    turned = dot(perm_t, mix, HIGH)
    lower_full = dot_nt(turned, upper_tri, HIGH)
    upper_full = dot_tn(lower_tri, turned, HIGH)
    rows, cols = iota((chans, chans), 0), iota((chans, chans), 1)
    lower_o[...] = jnp.where(rows > cols, lower_full, 0.0)
    upper_o[...] = jnp.where(cols > rows, upper_full, 0.0)
    diag = jnp.sum(jnp.where(rows == cols, upper_full, 0.0), axis=0, keepdims=True)
    jac_row = sums[0:1, base + 2 * hid : base + 2 * hid + chans]
    logs_o[...] = diag * jnp.exp(logs[...]) + jac_row
    for move in moves:
        move.wait()


def body(
    n,
    out_field,
    out_cot,
    jac_cot,
    mask,
    perm,
    lower_param,
    upper_param,
    log_scale,
    kern1,
    bias1,
    kern2,
    bias2,
):
    chans, count, sites = out_field.shape
    hid = kern1.shape[1]
    chips = n // 2
    perm_row = perm.reshape(1, chans)
    log_row = log_scale.reshape(1, chans)
    _, rows1 = block_rows(9 * hid, 9 * chans, FOLD1, n)
    _, rows2 = block_rows(9 * hid, 9 * hid, FOLD2, n)
    vmem = pl.BlockSpec(memory_space=pltpu.VMEM)
    shape = jax.ShapeDtypeStruct
    field = shape((chans, count, sites), F32)
    dma = pltpu.SemaphoreType.DMA
    norm = 1.0 / math.sqrt(count * sites * n)
    hbm = pl.BlockSpec(memory_space=pltpu.HBM)
    field_in, field_cot, gath1, grad2, small = pl.pallas_call(
        functools.partial(main_kernel, n, norm),
        out_shape=(
            field,
            field,
            shape((2, chips, rows1, 128), BF16),
            shape((2 * chans, hid, 81), F32),
            shape((8, 128), F32),
        ),
        in_specs=[hbm] * 12,
        out_specs=(vmem,) * 5,
        scratch_shapes=[
            pltpu.VMEM((chans, count, sites), F32),
            pltpu.VMEM((chans, count, sites), F32),
            pltpu.VMEM((count, sites), F32),
            pltpu.VMEM((count, sites), jnp.int32),
            pltpu.VMEM((1, chans), jnp.int32),
            pltpu.VMEM((chans, chans), F32),
            pltpu.VMEM((chans, chans), F32),
            pltpu.VMEM((1, chans), F32),
            pltpu.VMEM((hid, chans, 81), BF16),
            pltpu.VMEM((1, hid), F32),
            pltpu.VMEM((2 * chans, hid, 81), BF16),
            pltpu.VMEM((1, 2 * chans), F32),
            pltpu.VMEM((count + 4, chans, sites), BF16),
            pltpu.VMEM((count + 4, 9 * chans, sites), BF16),
            pltpu.VMEM((count + 2, 9 * hid, sites), BF16),
            pltpu.VMEM((count + 2, hid, sites), BF16),
            pltpu.VMEM((count + 2, hid, sites), BF16),
            pltpu.VMEM((9 * hid, 9 * chans), BF16),
            pltpu.VMEM((9 * chans, 9 * hid), BF16),
            pltpu.VMEM((9 * hid, 9 * hid), BF16),
            pltpu.VMEM((9 * hid, 9 * hid), BF16),
            pltpu.VMEM((81 * hid, chans), F32),
            pltpu.VMEM((81 * hid, hid), F32),
        ]
        + [pltpu.VMEM((2, chips, rows1, 128), BF16)] * 2
        + [pltpu.VMEM((chips, rows1, 128), BF16)] * 2
        + [pltpu.VMEM((2, chips, rows2, 128), BF16)] * 2
        + [pltpu.VMEM((chips, rows2, 128), BF16)] * 2
        + [pltpu.VMEM((8, 128), F32)] * 2
        + [pltpu.VMEM((chips, 8, 128), F32)]
        + [dma((2,))] * 3
        + [dma((6,))] * 2
        + [dma((chips,))] * 14
        + [dma((12,))],
        compiler_params=pltpu.CompilerParams(
            collective_id=0, has_side_effects=True, vmem_limit_bytes=VMEM_LIMIT
        ),
        name="block_backward",
    )(
        out_field,
        out_cot,
        jac_cot,
        mask,
        perm_row,
        lower_param,
        upper_param,
        log_row,
        kern1.transpose(1, 2, 0),
        bias1.reshape(1, hid),
        kern2.transpose(1, 2, 0),
        bias2.reshape(1, -1),
    )
    outs = pl.pallas_call(
        functools.partial(last_kernel, norm),
        out_shape=(
            field,
            field,
            shape((hid, chans, 81), F32),
            shape((1, hid), F32),
            shape((2 * chans, hid, 81), F32),
            shape((1, 2 * chans), F32),
            shape((chans, chans), F32),
            shape((chans, chans), F32),
            shape((1, chans), F32),
        ),
        in_specs=[vmem] * 9,
        out_specs=(hbm, hbm, vmem, vmem, hbm, vmem, vmem, vmem, vmem),
        scratch_shapes=[pltpu.VMEM((81 * hid, chans), F32), dma((3,))],
        compiler_params=pltpu.CompilerParams(vmem_limit_bytes=VMEM_LIMIT),
        name="unpack",
    )(
        field_in,
        field_cot,
        gath1.reshape(n * rows1, 128),
        grad2,
        small,
        perm_row,
        lower_param,
        upper_param,
        log_row,
    )
    return (
        outs[0],
        outs[1],
        outs[2].transpose(2, 0, 1),
        outs[3].reshape(-1),
        outs[4].transpose(2, 0, 1),
        outs[5].reshape(-1),
        outs[6],
        outs[7],
        outs[8].reshape(-1),
    )


def solution(mesh):
    split = ("groups", "ta")
    in_specs = (
        P(None, split, None),
        P(None, split, None),
        P(split, None),
        P(split, None),
    ) + (P(),) * 8
    out_specs = (
        P(None, split, None),
        P(None, split, None),
        P("groups", None, None),
        P("groups"),
        P("groups", None, None),
        P("groups"),
        P("groups", None),
        P("groups", None),
        P("groups"),
    )
    return jax.shard_map(
        functools.partial(body, mesh.shape["ta"]),
        mesh=mesh,
        in_specs=in_specs,
        out_specs=out_specs,
        check_vma=False,
    )
```

```python
import functools
import math

import jax
import jax.numpy as jnp
from jax import lax
from jax.experimental import pallas as pl
from jax.experimental.pallas import tpu as pltpu
from jax.sharding import PartitionSpec as P

LX = 8
LY = 8
LZ = 16
ROW = LY * LZ

HIGH = lax.Precision.HIGHEST
F32 = jnp.float32
BF16 = jnp.bfloat16
VMEM_LIMIT = 63 * 1024 * 1024


def dot(a, b, precision=None):
    return lax.dot_general(
        a, b, (((1,), (0,)), ((), ())), precision=precision, preferred_element_type=F32
    )


def dot_tn(a, b, precision=None):
    return lax.dot_general(
        a, b, (((0,), (0,)), ((), ())), precision=precision, preferred_element_type=F32
    )


def dot_nt(a, b, precision=None):
    return lax.dot_general(
        a, b, (((1,), (1,)), ((), ())), precision=precision, preferred_element_type=F32
    )


def split3(v):
    first = v.astype(BF16)
    rest = v - first.astype(F32)
    second = rest.astype(BF16)
    return first, second, (rest - second.astype(F32)).astype(BF16)


def mix_field(matrix, pieces):
    m1, m2, m3 = (m.astype(F32) for m in split3(matrix))
    x1, x2, x3 = pieces
    left = jnp.concatenate([m1, m1, m1, m2, m2, m3], axis=1).astype(BF16)
    return dot(left, jnp.concatenate([x1, x2, x3, x1, x2, x1], axis=0))


def iota(shape, dim):
    return lax.broadcasted_iota(jnp.int32, shape, dim)


def column(row):
    count = row.shape[1]
    same = iota((count, count), 0) == iota((count, count), 1)
    return jnp.sum(jnp.where(same, row, 0.0), axis=1, keepdims=True)


def substitute(strict, values, order):
    for j in order:
        values = values - strict[:, j : j + 1] * values[j : j + 1, :]
    return values


def factors(perm_row, lower_param, upper_param, log_row):
    chans = lower_param.shape[0]
    rows, cols = iota((chans, chans), 0), iota((chans, chans), 1)
    strict_low = jnp.where(rows > cols, lower_param, 0.0)
    strict_up = jnp.where(cols > rows, upper_param, 0.0)
    diag = column(jnp.exp(log_row))
    perm_t = jnp.where(rows == perm_row, 1.0, 0.0)
    lower_tri = strict_low + jnp.where(rows == cols, 1.0, 0.0)
    upper_tri = strict_up + jnp.where(rows == cols, diag, 0.0)
    return strict_low, strict_up, lower_tri, upper_tri, perm_t, diag


def to_tiles(v):
    return jnp.concatenate([v[:, x * ROW : (x + 1) * ROW] for x in range(LX)], axis=0)


def to_lanes(v):
    chans = v.shape[0] // LX
    return jnp.concatenate([v[x * chans : (x + 1) * chans] for x in range(LX)], axis=1)


def shift_z(v, off):
    if off == 0:
        return v
    z = iota(v.shape, 1) % LZ
    if off > 0:
        return jnp.where(z == LZ - 1, pltpu.roll(v, LZ - 1, 1), pltpu.roll(v, ROW - 1, 1))
    return jnp.where(z == 0, pltpu.roll(v, ROW - LZ + 1, 1), pltpu.roll(v, 1, 1))


def shift_y(v, off):
    if off == 0:
        return v
    return pltpu.roll(v, (ROW - off * LZ) % ROW, 1)


def shift_x(v, off):
    if off == 0:
        return v
    if off > 0:
        return jnp.concatenate([v[:, ROW:], v[:, :ROW]], axis=1)
    return jnp.concatenate([v[:, -ROW:], v[:, :-ROW]], axis=1)


def store_plane_stack(ref, slot, v):
    chans = v.shape[0]
    tiles = to_tiles(v)
    along_z = [shift_z(tiles, e) for e in (-1, 0, 1)]
    for c in (-1, 0, 1):
        for e in (-1, 0, 1):
            k = 3 * (c + 1) + e + 1
            piece = to_lanes(shift_y(along_z[e + 1], c)).astype(BF16)
            ref[slot, k * chans : (k + 1) * chans, :] = piece


def unstack_plane(q):
    chans = q.shape[0] // 9
    total = None
    for e in (-1, 0, 1):
        along = None
        for c in (-1, 0, 1):
            k = 3 * (c + 1) + e + 1
            piece = shift_y(to_tiles(q[k * chans : (k + 1) * chans]), -c)
            along = piece if along is None else along + piece
        along = shift_z(along, -e)
        total = along if total is None else total + along
    return to_lanes(total)


def valid_taps(source, count):
    taps = [a for a in (-1, 0, 1) if 0 <= source - a < count]
    return taps[0], taps[-1] + 1


def add_forward(outs, weight, stack, source):
    first, end = valid_taps(source, len(outs))
    hid = weight.shape[0] // 9
    prod = dot(weight[3 * hid * (first + 1) : 3 * hid * (end + 1), :], stack)
    for a in range(first, end):
        for b in (-1, 0, 1):
            lo = (3 * (a - first) + b + 1) * hid
            piece = shift_x(prod[lo : lo + hid], b)
            t = source - a
            outs[t] = piece if outs[t] is None else outs[t] + piece


def spread_stack(slices, taps):
    return jnp.concatenate(
        [shift_x(slices[i], -b) for i in range(len(taps)) for b in (-1, 0, 1)], axis=0
    )


def kernel_grads(cot, stacks, count):
    blocks = {}
    for source in range(-1, count + 1):
        first, end = valid_taps(source, count)
        taps = list(range(first, end))
        left = spread_stack([cot[source - a] for a in taps], taps)
        prod = dot_nt(left, stacks(source))
        for i, a in enumerate(taps):
            size = left.shape[0] // len(taps)
            part = prod[i * size : (i + 1) * size]
            blocks[a] = part if a not in blocks else blocks[a] + part
    return jnp.concatenate([blocks[a] for a in (-1, 0, 1)], axis=0)


def to_blocks(grad, fold):
    rows, cols = grad.shape
    full = cols // 128
    rest = cols - full * 128
    parts = [grad[:, i * 128 : (i + 1) * 128] for i in range(full)]
    tail = grad[:, full * 128 :]
    each = rows // fold
    tails = [tail[i * each : (i + 1) * each] for i in range(fold)]
    tails.append(jnp.zeros((each, 128 - rest * fold), F32))
    parts.append(jnp.concatenate(tails, axis=1))
    return jnp.concatenate(parts, axis=0)


def from_blocks(packed, rows, cols, fold):
    full = cols // 128
    rest = cols - full * 128
    each = rows // fold
    parts = [packed[i * rows : (i + 1) * rows] for i in range(full)]
    last = packed[full * rows : full * rows + each]
    tail = jnp.concatenate([last[:, i * rest : (i + 1) * rest] for i in range(fold)], axis=0)
    return jnp.concatenate(parts + [tail], axis=1)


def block_rows(rows, cols, fold, n):
    total = (cols // 128) * rows + rows // fold
    blocks = -(-total // 16)
    return total, 16 * -(-blocks // n)


FOLD2 = 1


def unpack_grad(packed, taps, hid, ins, fold, norm):
    grid = from_blocks(packed.astype(F32) * norm, 9 * hid, 9 * ins, fold)
    return tap_rows(grid, taps, hid, ins).reshape(hid, ins, 81)


def tap_rows(grid, taps, hid, ins):
    for k in range(9):
        for x in range(9):
            start = (9 * x + k) * hid
            taps[start : start + hid, :] = grid[
                x * hid : (x + 1) * hid, k * ins : (k + 1) * ins
            ]
    flat = jnp.concatenate([taps[pl.ds(o, 81, stride=hid), :] for o in range(hid)], axis=1)
    return flat.T


def main_kernel(n, norm, *refs):
    given, refs = refs[:12], refs[12:]
    held, rest = refs[9:21], refs[:9] + refs[21:-1]
    in_sem = refs[-1]
    loads = [
        pltpu.make_async_copy(src, dst, in_sem.at[i])
        for i, (src, dst) in enumerate(zip(given, held))
    ]
    for i in (5, 6, 7, 4, 0, 3, 8, 10, 1, 2, 9, 11):
        loads[i].start()
    compute(n, norm, loads, *held, *rest)


def compute(
    n,
    norm,
    loads,
    out_field,
    out_cot,
    jac,
    mask,
    perm,
    lower,
    upper,
    logs,
    kern1,
    bias1,
    kern2,
    bias2,
    field_in_o,
    field_cot_o,
    kern1_o,
    bias1_o,
    kern2_o,
    bias2_o,
    lower_o,
    upper_o,
    logs_o,
    frozen,
    stack1,
    stack2,
    ncot,
    pcot,
    w1,
    w1t,
    w2,
    w2t,
    taps1,
    taps2,
    send1,
    gath1,
    paired1,
    recv1,
    send2,
    gath2,
    paired2,
    recv2,
    small_mine,
    small_other,
    small_all,
    p1_sem,
    p2_sem,
    ps_sem,
    halo_send,
    halo_recv,
    s1_send,
    s1_recv,
    s2_send,
    s2_recv,
    g1_send,
    g1_recv,
    g2_send,
    g2_recv,
    sm_send,
    sm_recv,
    f1_send,
    f1_recv,
    f2_send,
    f2_recv,
):
    me = lax.axis_index("ta")
    chans, count, sites = out_field.shape
    hid = kern1.shape[0]
    right, left = lax.rem(me + 1, n), lax.rem(me + n - 1, n)
    chips = n // 2
    chip, core = me // 2, lax.rem(me, 2)
    other = 1 - core
    partner = 2 * chip + other

    barrier = pltpu.get_barrier_semaphore()

    def greet(k, carry):
        pl.semaphore_signal(barrier, inc=1, device_id={"ta": lax.rem(me + k, n)})
        return carry

    lax.fori_loop(1, n, greet, 0)

    for i in (4, 5, 6, 7):
        loads[i].wait()
    strict_low, strict_up, lower_tri, upper_tri, perm_t, diag = factors(
        perm[...], lower[...], upper[...], logs[...]
    )
    solved = substitute(strict_low, perm_t, range(chans))
    unmixer = substitute(strict_up / diag, solved / diag, range(chans - 1, -1, -1))
    mixer_t = dot_tn(dot(lower_tri, upper_tri, HIGH), perm_t, HIGH)

    for i in (0, 3):
        loads[i].wait()
    keep = [mask[t : t + 1, :].astype(F32) for t in range(count)]
    coupled = [mix_field(unmixer, split3(out_field[:, t, :])) for t in range(count)]
    for t in range(count):
        frozen[2 + t] = (keep[t] * coupled[t]).astype(BF16)

    pl.semaphore_wait(barrier, n - 1)

    def halo(index, src, dst, where):
        return pltpu.make_async_remote_copy(
            src_ref=src,
            dst_ref=dst,
            send_sem=halo_send.at[index],
            recv_sem=halo_recv.at[index],
            device_id={"ta": where},
        )

    def exchange(base, buf, width):
        up = halo(base, buf.at[pl.ds(count, width)], buf.at[pl.ds(0, width)], right)
        down = halo(
            base + 1, buf.at[pl.ds(width, width)], buf.at[pl.ds(width + count, width)], left
        )
        up.start()
        down.start()
        return up, down

    first_halo = exchange(0, frozen, 2)

    def remote(src, dst, send_sem, recv_sem, where):
        return pltpu.make_async_remote_copy(
            src_ref=src,
            dst_ref=dst,
            send_sem=send_sem,
            recv_sem=recv_sem,
            device_id={"ta": where},
        )

    def ahead(k):
        return lax.rem(chip + k, chips)

    def behind(k):
        return lax.rem(chip + chips - k, chips)

    def each(step):
        def run(k, carry):
            step(k)
            return carry

        lax.fori_loop(1, chips, run, 0)

    def pair_copy(send, paired, sems):
        return remote(send.at[other], paired, sems.at[0], sems.at[1], partner)

    def load_send(send, packed):
        rows = send.shape[2]
        for p in range(n):
            send[p // chips, p % chips] = packed[p * rows : (p + 1) * rows]

    def pair_sum(send, paired):
        paired[...] = (send[core].astype(F32) + paired[...].astype(F32)).astype(BF16)

    def scatter_copy(paired, recv, s_sem, r_sem, k):
        return remote(
            paired.at[ahead(k)], recv.at[k], s_sem.at[k], r_sem.at[k], 2 * ahead(k) + core
        )

    def scatter(*refs):
        each(lambda k: scatter_copy(*refs, k).start())

    def collect(paired, recv, s_sem, r_sem):
        def step(k, total):
            scatter_copy(paired, recv, s_sem, r_sem, k).wait()
            return total + recv[k].astype(F32)

        return lax.fori_loop(1, chips, step, paired[chip].astype(F32)).astype(BF16)

    def gather_copy(buf, s_sem, r_sem, k, at):
        return remote(
            buf.at[core, chip], buf.at[core, at], s_sem.at[k], r_sem.at[k], 2 * ahead(k) + core
        )

    def forward_copy(buf, f_send, f_recv, k, to):
        return remote(
            buf.at[core, behind(k)], buf.at[to, behind(k)], f_send.at[k], f_recv.at[k], partner
        )

    def gather(buf, s_sem, r_sem, f_send, f_recv):
        forward_copy(buf, f_send, f_recv, 0, core).start()
        each(lambda k: gather_copy(buf, s_sem, r_sem, k, chip).start())

    def gather_forward(buf, s_sem, r_sem, f_send, f_recv):
        def step(k):
            gather_copy(buf, s_sem, r_sem, k, behind(k)).wait_recv()
            forward_copy(buf, f_send, f_recv, k, core).start()

        each(step)

    def gather_done(buf, s_sem, r_sem, f_send, f_recv):
        def step(k):
            gather_copy(buf, s_sem, r_sem, k, chip).wait_send()
            forward_copy(buf, f_send, f_recv, k, core).wait_send()
            forward_copy(buf, f_send, f_recv, k, other).wait_recv()

        forward_copy(buf, f_send, f_recv, 0, core).wait_send()
        forward_copy(buf, f_send, f_recv, 0, other).wait_recv()
        each(step)

    for i in (8, 10, 1, 2, 9, 11):
        loads[i].wait()
    for kern, taps, w, wt in ((kern1, taps1, w1, w1t), (kern2, taps2, w2, w2t)):
        ins = kern.shape[1]
        flat = kern[...].astype(F32).reshape(hid * ins, 81).T
        for o in range(hid):
            taps[pl.ds(o, 81, stride=hid), :] = flat[:, o * ins : (o + 1) * ins]
        split = taps[...].reshape(9, 9, hid, ins)
        wide = jnp.concatenate(
            [split[:, k].reshape(9 * hid, ins) for k in range(9)], axis=1
        )
        w[...] = wide.astype(BF16)
        wt[...] = wide.T.astype(BF16)

    cot_pieces = [split3(out_cot[:, t, :]) for t in range(count)]
    coupled_cot = [mix_field(mixer_t, cot_pieces[t]) for t in range(count)]
    wide_mix = None
    for t in range(count):
        term = dot_nt(
            jnp.concatenate(cot_pieces[t], axis=0),
            jnp.concatenate(split3(coupled[t]), axis=0),
        )
        wide_mix = term if wide_mix is None else wide_mix + term
    mix = None
    for i, j in ((2, 0), (1, 1), (0, 2), (1, 0), (0, 1), (0, 0)):
        term = wide_mix[i * chans : (i + 1) * chans, j * chans : (j + 1) * chans]
        mix = term if mix is None else mix + term
    jac_sum = jnp.sum(jnp.sum(jac[...], axis=1, keepdims=True), axis=0, keepdims=True)

    hidden_pre = [None] * (count + 2)
    for slot in range(2, count + 2):
        store_plane_stack(stack1, slot, frozen[slot].astype(F32))
        add_forward(hidden_pre, w1, stack1[slot], slot - 1)
    for copy in first_halo:
        copy.wait()
    for slot in [0, 1] + [count + 2, count + 3]:
        store_plane_stack(stack1, slot, frozen[slot].astype(F32))
        add_forward(hidden_pre, w1, stack1[slot], slot - 1)

    bias1_col = column(bias1[...])
    bias2_col = column(bias2[...])
    net = [None] * count
    hidden_mid = []
    for slot in range(count + 2):
        hidden = jnp.tanh(hidden_pre[slot] + bias1_col).astype(BF16).astype(F32)
        if 1 <= slot <= count:
            hidden_mid.append(hidden)
        store_plane_stack(stack2, slot, hidden)
        add_forward(net, w2, stack2[slot], slot - 1)

    growth = []
    cots = []
    for t in range(count):
        net_t = net[t] + bias2_col
        scale = jnp.tanh(net_t[:chans])
        shift = net_t[chans:]
        free = 1.0 - keep[t]
        grow = jnp.exp(scale)
        growth.append(grow)
        fin = keep[t] * coupled[t] + free * (coupled[t] - shift) * jnp.exp(-scale)
        field_in_o[:, t, :] = fin
        scale_cot = free * (coupled_cot[t] * fin * grow + jac[t : t + 1, :])
        cot = jnp.concatenate(
            [scale_cot * (1.0 - scale * scale), free * coupled_cot[t]], axis=0
        ).astype(BF16)
        ncot[1 + t] = cot
        cots.append(cot)
    second_halo = exchange(2, ncot, 1)

    grads2 = kernel_grads(cots, lambda s: stack2[s + 1], count)
    total2, rows2 = block_rows(9 * hid, 9 * hid, FOLD2, n)
    packed2 = to_blocks(grads2, FOLD2)
    packed2 = jnp.concatenate(
        [packed2, jnp.zeros((n * rows2 - total2, 128), F32)], axis=0
    ).astype(BF16)
    load_send(send2, packed2)
    pair2 = pair_copy(send2, paired2, p2_sem)
    pair2.start()

    ones = jnp.ones((8, sites), BF16)
    bias2_row = sum(dot_nt(ones, c) for c in cots)

    for copy in second_halo:
        copy.wait()
    pres = []
    for t in range(count):
        taps = (-1, 0, 1)
        wide = spread_stack([ncot[1 + t - a] for a in taps], taps)
        hidden_cot = unstack_plane(dot(w2t[...], wide))
        pre = (hidden_cot * (1.0 - hidden_mid[t] * hidden_mid[t])).astype(BF16)
        pcot[1 + t] = pre
        pres.append(pre)
    third_halo = exchange(4, pcot, 1)

    pair2.wait()
    pair_sum(send2, paired2)
    scatter(paired2, recv2, s2_send, s2_recv)

    grads1 = kernel_grads(pres, lambda s: stack1[s + 2], count)
    rows1 = send1.shape[2]
    ordered = tap_rows(grads1, taps1, hid, chans)
    packed1 = jnp.concatenate([ordered, jnp.zeros((hid * chans, 47), F32)], axis=1)
    if n * rows1 > hid * chans:
        packed1 = jnp.concatenate(
            [packed1, jnp.zeros((n * rows1 - hid * chans, 128), F32)], axis=0
        )
    packed1 = packed1.astype(BF16)
    load_send(send1, packed1)
    pair1 = pair_copy(send1, paired1, p1_sem)
    pair1.start()

    bias1_row = sum(dot_nt(ones, c) for c in pres)
    small_mine[...] = jnp.concatenate(
        [mix[:8], mix[8:], bias1_row, bias2_row, jnp.broadcast_to(jac_sum, (8, 32))], axis=1
    )
    pair_small = remote(small_mine, small_other, ps_sem.at[0], ps_sem.at[1], partner)
    pair_small.start()

    gath2[core, chip] = collect(paired2, recv2, s2_send, s2_recv)
    gather(gath2, g2_send, g2_recv, f2_send, f2_recv)

    pair1.wait()
    pair_sum(send1, paired1)
    scatter(paired1, recv1, s1_send, s1_recv)
    pair_small.wait()
    small_all[chip] = small_mine[...] + small_other[...]

    def small_copy(k, at):
        return remote(
            small_all.at[chip],
            small_all.at[at],
            sm_send.at[k],
            sm_recv.at[k],
            2 * ahead(k) + core,
        )

    each(lambda k: small_copy(k, chip).start())

    for copy in third_halo:
        copy.wait()
    for t in range(count):
        taps = (-1, 0, 1)
        wide = spread_stack([pcot[1 + t - a] for a in taps], taps)
        frozen_cot = unstack_plane(dot(w1t[...], wide))
        free = 1.0 - keep[t]
        field_cot_o[:, t, :] = (
            keep[t] * (coupled_cot[t] + frozen_cot) + free * coupled_cot[t] * growth[t]
        )

    gath1[core, chip] = collect(paired1, recv1, s1_send, s1_recv)
    gather(gath1, g1_send, g1_recv, f1_send, f1_recv)

    gather_forward(gath2, g2_send, g2_recv, f2_send, f2_recv)
    gather_done(gath2, g2_send, g2_recv, f2_send, f2_recv)
    kern2_o[...] = unpack_grad(
        gath2[...].reshape(n * rows2, 128), taps2, hid, hid, FOLD2, norm
    )

    def small_done(k):
        small_copy(k, chip).wait_send()
        small_copy(k, behind(k)).wait_recv()

    each(small_done)
    small_sum = lax.fori_loop(
        0, chips, lambda k, total: total + small_all[k], jnp.zeros(small_mine.shape, F32)
    )

    sums = small_sum * norm
    total_mix = jnp.concatenate([sums[:, :chans], sums[:, chans : 2 * chans]], axis=0)
    base = 2 * chans
    bias1_o[...] = sums[0:1, base : base + hid]
    bias2_o[...] = sums[0:1, base + hid : base + 2 * hid]
    turned = dot(perm_t, total_mix, HIGH)
    lower_full = dot_nt(turned, upper_tri, HIGH)
    upper_full = dot_tn(lower_tri, turned, HIGH)
    rows, cols = iota((chans, chans), 0), iota((chans, chans), 1)
    lower_o[...] = jnp.where(rows > cols, lower_full, 0.0)
    upper_o[...] = jnp.where(cols > rows, upper_full, 0.0)
    diag = jnp.sum(jnp.where(rows == cols, upper_full, 0.0), axis=0, keepdims=True)
    jac_row = sums[0:1, base + 2 * hid : base + 2 * hid + chans]
    logs_o[...] = diag * jnp.exp(logs[...]) + jac_row

    gather_forward(gath1, g1_send, g1_recv, f1_send, f1_recv)
    gather_done(gath1, g1_send, g1_recv, f1_send, f1_recv)
    done1 = gath1[...].reshape(n * rows1, 128)[: hid * chans, :81].astype(F32) * norm
    kern1_o[...] = done1.reshape(hid, chans, 81)


def last_kernel(*refs):
    out_sem = refs[18]
    moves = [
        pltpu.make_async_copy(refs[i], refs[9 + i], out_sem.at[i]) for i in range(9)
    ]
    for i in (4, 2, 0, 1, 3, 5, 6, 7, 8):
        moves[i].start()
    for move in moves:
        move.wait()


def body(
    n,
    out_field,
    out_cot,
    jac_cot,
    mask,
    perm,
    lower_param,
    upper_param,
    log_scale,
    kern1,
    bias1,
    kern2,
    bias2,
):
    chans, count, sites = out_field.shape
    hid = kern1.shape[1]
    chips = n // 2
    perm_row = perm.reshape(1, chans)
    log_row = log_scale.reshape(1, chans)
    rows1 = 16 * -(-(hid * chans // 16) // n)
    _, rows2 = block_rows(9 * hid, 9 * hid, FOLD2, n)
    vmem = pl.BlockSpec(memory_space=pltpu.VMEM)
    shape = jax.ShapeDtypeStruct
    field = shape((chans, count, sites), F32)
    dma = pltpu.SemaphoreType.DMA
    norm = 1.0 / math.sqrt(count * sites * n)
    hbm = pl.BlockSpec(memory_space=pltpu.HBM)
    results = (
        field,
        field,
        shape((hid, chans, 81), F32),
        shape((1, hid), F32),
        shape((2 * chans, hid, 81), F32),
        shape((1, 2 * chans), F32),
        shape((chans, chans), F32),
        shape((chans, chans), F32),
        shape((1, chans), F32),
    )
    found = pl.pallas_call(
        functools.partial(main_kernel, n, norm),
        out_shape=results,
        in_specs=[hbm] * 12,
        out_specs=(vmem,) * 9,
        scratch_shapes=[
            pltpu.VMEM((chans, count, sites), F32),
            pltpu.VMEM((chans, count, sites), F32),
            pltpu.VMEM((count, sites), F32),
            pltpu.VMEM((count, sites), jnp.int32),
            pltpu.VMEM((1, chans), jnp.int32),
            pltpu.VMEM((chans, chans), F32),
            pltpu.VMEM((chans, chans), F32),
            pltpu.VMEM((1, chans), F32),
            pltpu.VMEM((hid, chans, 81), BF16),
            pltpu.VMEM((1, hid), F32),
            pltpu.VMEM((2 * chans, hid, 81), BF16),
            pltpu.VMEM((1, 2 * chans), F32),
            pltpu.VMEM((count + 4, chans, sites), BF16),
            pltpu.VMEM((count + 4, 9 * chans, sites), BF16),
            pltpu.VMEM((count + 2, 9 * hid, sites), BF16),
            pltpu.VMEM((count + 2, hid, sites), BF16),
            pltpu.VMEM((count + 2, hid, sites), BF16),
            pltpu.VMEM((9 * hid, 9 * chans), BF16),
            pltpu.VMEM((9 * chans, 9 * hid), BF16),
            pltpu.VMEM((9 * hid, 9 * hid), BF16),
            pltpu.VMEM((9 * hid, 9 * hid), BF16),
            pltpu.VMEM((81 * hid, chans), F32),
            pltpu.VMEM((81 * hid, hid), F32),
        ]
        + [pltpu.VMEM((2, chips, rows1, 128), BF16)] * 2
        + [pltpu.VMEM((chips, rows1, 128), BF16)] * 2
        + [pltpu.VMEM((2, chips, rows2, 128), BF16)] * 2
        + [pltpu.VMEM((chips, rows2, 128), BF16)] * 2
        + [pltpu.VMEM((8, 128), F32)] * 2
        + [pltpu.VMEM((chips, 8, 128), F32)]
        + [dma((2,))] * 3
        + [dma((6,))] * 2
        + [dma((chips,))] * 14
        + [dma((12,))],
        compiler_params=pltpu.CompilerParams(
            collective_id=0, has_side_effects=True, vmem_limit_bytes=VMEM_LIMIT
        ),
        name="block_backward",
    )(
        out_field,
        out_cot,
        jac_cot,
        mask,
        perm_row,
        lower_param,
        upper_param,
        log_row,
        kern1.transpose(1, 2, 0),
        bias1.reshape(1, hid),
        kern2.transpose(1, 2, 0),
        bias2.reshape(1, -1),
    )
    outs = pl.pallas_call(
        last_kernel,
        out_shape=results,
        in_specs=[hbm] * 9,
        out_specs=(hbm,) * 9,
        scratch_shapes=[dma((9,))],
        compiler_params=pltpu.CompilerParams(vmem_limit_bytes=VMEM_LIMIT),
        name="deliver",
    )(*found)
    return (
        outs[0],
        outs[1],
        outs[2].transpose(2, 0, 1),
        outs[3].reshape(-1),
        outs[4].transpose(2, 0, 1),
        outs[5].reshape(-1),
        outs[6],
        outs[7],
        outs[8].reshape(-1),
    )


def solution(mesh):
    split = ("groups", "ta")
    in_specs = (
        P(None, split, None),
        P(None, split, None),
        P(split, None),
        P(split, None),
    ) + (P(),) * 8
    out_specs = (
        P(None, split, None),
        P(None, split, None),
        P("groups", None, None),
        P("groups"),
        P("groups", None, None),
        P("groups"),
        P("groups", None),
        P("groups", None),
        P("groups"),
    )
    return jax.shard_map(
        functools.partial(body, mesh.shape["ta"]),
        mesh=mesh,
        in_specs=in_specs,
        out_specs=out_specs,
        check_vma=False,
    )
```
